256 devices in a mesh: dp: 16 (over z, core), expert: 16 (over x, y).
Axes of the slice: x: 4, y: 4, z: 8, core: 2. Of those that a mesh axis runs over, the one named last changes fastest.
Arguments:
- hidden: bfloat16 [36864, 2048], P(('dp', 'expert')), may hold values from -6 to 6
- w_gate: bfloat16 [32, 2048, 384], P('expert'), may hold values from -0.125 to 0.125
- w_up: bfloat16 [32, 2048, 384], P('expert'), may hold values from -0.125 to 0.125
- w_down: bfloat16 [32, 384, 2048], P('expert'), may hold values from -0.3125 to 0.3125
- expert_ids: int32 [36864, 8], P(('dp', 'expert')), may hold values from 0 to 31, as said below
- route_weight: bfloat16 [36864, 8], P(('dp', 'expert')), may hold values from 0.029907227 to 0.29882812
- seq_len: int32 [768], P(('dp', 'expert')), may hold values from 36 to 48, as said below
- positive: int32 [256], P(('dp', 'expert')), may hold values from 0 to 31
Outputs:
- query_loss: float32 [256], P(('dp', 'expert'))
- grad_gate: float32 [32, 2048, 384], P('expert', 'dp')
- grad_up: float32 [32, 2048, 384], P('expert', 'dp')
- grad_down: float32 [32, 384, 2048], P('expert', None, 'dp')
The draws below stay inside these ranges and needn't reach their ends.
Inputs may be any that keep to these rules, and one draw needn't show every extreme that they name: `expert_ids`: among the valid token slots of one block, no expert is named by more than 38 of them; the ids of slots that are not valid carry no data. `seq_len`: valid tokens of a sequence of 48 slots; some blocks hold only full sequences, and blocks differ in how full their sequences are.
All inputs are finite; a program needn't handle non-finite values.
Results may differ from the reference program's by a relative error of at most 0.03.
Values may be sent and summed in bfloat16 or wider, within the bound.
No kernel may reach another device: no remote copies, remote signals or barrier semaphores. Data moves between devices by JAX's collectives and lax.ppermute only.
A program may use at most 128 MiB of HBM per device.

```python
import math
import jax
import jax.numpy as jnp
from jax import lax

D = 2048
FF = 384
TOP = 8
LEN = 48
QRY_DEV = 1
PSG_DEV = 2
SEQ_DEV = 3
TOK_DEV = 144
EXPERTS = 32
CAP = 38
TOKENS = 36864
SEQS = 768
QUERIES = 256
N_DP = 16
N_EXPERT = 16


def draw_lengths(key):
    key_level, key_drop = jax.random.split(key)
    blocks = SEQS // SEQ_DEV
    levels = jax.random.randint(key_level, (blocks, 1), 0, 3)
    levels = levels.at[0, 0].set(0)
    most_drop = jnp.where(levels == 2, LEN // 4, levels * (LEN // 8))
    dropped = jax.random.randint(key_drop, (blocks, SEQ_DEV), 0, most_drop + 1)
    lengths = LEN - dropped
    lengths = lengths.at[blocks - 1, 0].set(LEN - LEN // 4)
    return lengths.astype(jnp.int32)


def draw_seq_len(key, part):
    lengths = draw_lengths(key)
    return lengths.reshape(SEQS).astype(jnp.int32)


def spread_loads(is_hot, spread, label_order, remain, stretch):
    weights = jnp.where(is_hot, 0, 16 + spread * stretch // 48)
    ordered = jnp.take_along_axis(weights, label_order, axis=1)
    running = jnp.cumsum(ordered, axis=1)
    bounds = remain[:, None] * running // running[:, -1:]
    starts = jnp.concatenate([jnp.zeros_like(bounds[:, :1]), bounds[:, :-1]], axis=1)
    return bounds - starts


def draw_expert_ids(key, part):
    lengths = draw_lengths(key)
    key = jax.random.fold_in(key, 11)
    subkeys = jax.random.split(key, 9)
    blocks = lengths.shape[0]
    groups = blocks // N_EXPERT
    positions = jnp.arange(TOK_DEV, dtype=jnp.int32)
    live_slot = (positions % LEN)[None, :] < lengths[:, positions // LEN]
    counts = jnp.sum(live_slot.astype(jnp.int32), axis=1)
    ceiling = jnp.minimum(counts, CAP)
    labels = jnp.arange(EXPERTS, dtype=jnp.int32)
    group_of = jnp.arange(blocks, dtype=jnp.int32) // N_EXPERT
    group_hot = jax.random.randint(subkeys[0], (groups,), 0, EXPERTS)
    block_hot = jax.random.randint(subkeys[1], (blocks,), 0, EXPERTS)
    shared = jax.random.randint(subkeys[2], (groups,), 0, 2).at[0].set(1)
    first_hot = jnp.where(shared[group_of] == 1, group_hot[group_of], block_hot)
    second_pick = jax.random.randint(subkeys[3], (blocks,), 0, EXPERTS - 1)
    second_hot = second_pick + (second_pick >= first_hot).astype(jnp.int32)
    is_hot = jnp.logical_or(labels[None, :] == first_hot[:, None], labels[None, :] == second_hot[:, None])
    spread = jax.random.randint(subkeys[4], (blocks, EXPERTS), 0, 49)
    shuffle = jax.random.randint(subkeys[5], (blocks, EXPERTS), 0, 1 << 16) * EXPERTS + labels[None, :]
    label_order = jnp.argsort(shuffle, axis=1).astype(jnp.int32)
    remain = counts * TOP - 2 * ceiling
    chosen = spread_loads(is_hot, spread, label_order, remain, 0)
    for stretch in (8, 24, 48):
        attempt = spread_loads(is_hot, spread, label_order, remain, stretch)
        fitting = jnp.max(attempt, axis=1, keepdims=True) <= ceiling[:, None]
        chosen = jnp.where(fitting, attempt, chosen)
    hot_order = jnp.take_along_axis(is_hot.astype(jnp.int32), label_order, axis=1)
    loads = chosen + hot_order * ceiling[:, None]
    ticket_ends = jnp.cumsum(loads, axis=1)
    row_noise = jax.random.randint(subkeys[6], (blocks, TOK_DEV), 0, 1 << 16) * TOK_DEV + positions[None, :]
    row_order = jnp.argsort(jnp.where(live_slot, row_noise, row_noise + (1 << 28)), axis=1)
    row_rank = jnp.argsort(row_order, axis=1).astype(jnp.int32)
    columns = jnp.arange(TOP, dtype=jnp.int32)
    tickets = row_rank[:, :, None] + columns[None, None, :] * counts[:, None, None]
    position_of = jnp.sum((ticket_ends[:, None, None, :] <= tickets[:, :, :, None]).astype(jnp.int32), axis=3)
    position_of = jnp.minimum(position_of, EXPERTS - 1)
    routed_ids = jnp.take_along_axis(label_order, position_of.reshape(blocks, TOK_DEV * TOP), axis=1).reshape(blocks, TOK_DEV, TOP)
    padded_start = jax.random.randint(subkeys[7], (blocks, TOK_DEV), 0, EXPERTS)
    padded_ids = (padded_start[:, :, None] + columns[None, None, :]) % EXPERTS
    expert_pick = jnp.where(live_slot[:, :, None], routed_ids, padded_ids)
    rotation = jax.random.randint(subkeys[8], (blocks, TOK_DEV), 0, TOP)
    expert_pick = jnp.take_along_axis(expert_pick, (columns[None, None, :] + rotation[:, :, None]) % TOP, axis=2)
    return expert_pick.reshape(TOKENS, TOP).astype(jnp.int32)


def plant(array, rng, smallest, high):
    dims = array.shape
    spot = [jax.random.randint(jax.random.fold_in(rng, axis), (), 0, dims[axis]) for axis in range(len(dims))]
    array = array.at[tuple(spot)].set(smallest)
    longest = dims.index(max(dims))
    spot[longest] = (spot[longest] + 1) % dims[longest]
    return array.at[tuple(spot)].set(high)


def level_of(key, dims, cuts, smallest, high):
    def one(axis_at, shards_of):
        heights = jax.random.uniform(jax.random.fold_in(jax.random.fold_in(key, 6), axis_at), (shards_of,), jnp.float32, smallest / len(cuts), high / len(cuts))
        return jnp.repeat(jnp.exp(heights), dims[axis_at] // shards_of).reshape((-1,) + (1,) * (len(dims) - axis_at - 1))

    level = one(*cuts[0])
    for cut in cuts[1:]:
        level = level * one(*cut)
    return level


def noise(key, shape, scale, reach, pieces=(), kind=jnp.bfloat16):
    array = scale * jax.random.normal(key, shape, jnp.float32)
    if pieces:
        array = array * level_of(key, shape, pieces, -0.22, 0.18)
    return jnp.clip(array, -reach, reach).astype(kind)


def setup_inputs(seed: int = 0) -> dict:
    seeds = jax.random.split(jax.random.key(seed), 9)
    return {
        "hidden": noise(seeds[0], (TOKENS, D), 1.0, 6.0, ((0, 256),)),
        "w_gate": noise(seeds[1], (EXPERTS, D, FF), D ** -0.5, 0.125, ((0, 16),)),
        "w_up": noise(seeds[2], (EXPERTS, D, FF), D ** -0.5, 0.125, ((0, 16),)),
        "w_down": noise(seeds[3], (EXPERTS, FF, D), FF ** -0.5, 0.3125, ((0, 16),)),
        "expert_ids": draw_expert_ids(jax.random.fold_in(seeds[8], 71), 0),
        "route_weight": jnp.clip(jnp.exp(math.log(0.29882812) - 2.30176843 * jax.random.uniform(seeds[5], (TOKENS, TOP), jnp.float32) ** level_of(seeds[5], (TOKENS, TOP), ((0, 256),), -0.2, 0.2)), 0.029907227, 0.29882812).astype(jnp.bfloat16),
        "seq_len": draw_seq_len(jax.random.fold_in(seeds[8], 71), 0),
        "positive": plant(jax.random.randint(seeds[7], (QUERIES,), 0, PSG_DEV * N_DP), jax.random.fold_in(seeds[7], 1), 0, (PSG_DEV * N_DP) - 1).astype(jnp.int32),
    }


inv_temp = 20.0
loss_scale = 128.0
norm_eps = 1e-06

def rounded(values):
    return lax.optimization_barrier(values.astype(jnp.bfloat16)).astype(jnp.float32)

def silu_parts(gate_pre):
    sigma = jax.nn.sigmoid(gate_pre)
    return (gate_pre * sigma, sigma * (1.0 + gate_pre * (1.0 - sigma)))

def slot_tables(expert_ids, route_weight, seq_len, experts, capacity):
    tok_count, top_count = expert_ids.shape
    seq_count = seq_len.shape[0]
    length = tok_count // seq_count
    position = jnp.arange(tok_count, dtype=jnp.int32)
    member = position[:, None] // length == jnp.arange(seq_count, dtype=jnp.int32)[None, :]
    bound = lax.optimization_barrier(jnp.sum(jnp.where(member, seq_len[None, :], 0), axis=1))
    valid = position % length < bound
    member_live = jnp.logical_and(member, valid[:, None])
    inverse = 1.0 / seq_len.astype(jnp.float32)
    pool = jnp.where(member_live, inverse[None, :], 0.0).astype(jnp.float32)
    hits = jnp.logical_and(expert_ids[:, :, None] == jnp.arange(experts, dtype=jnp.int32)[None, None, :], valid[:, None, None])
    flat = hits.reshape(tok_count * top_count, experts).astype(jnp.int32)
    before = jnp.cumsum(flat, axis=0) - flat
    place = lax.optimization_barrier(jnp.sum(before * flat, axis=1)).reshape(tok_count, top_count)
    slot = expert_ids * capacity + place
    pick = jnp.logical_and(slot[:, :, None] == jnp.arange(experts * capacity, dtype=jnp.int32)[None, None, :], valid[:, None, None])
    dispatch = lax.optimization_barrier(jnp.sum(pick.astype(jnp.float32), axis=1)).astype(jnp.bfloat16)
    combine = lax.optimization_barrier(jnp.sum(jnp.where(pick, route_weight.astype(jnp.float32)[:, :, None], 0.0), axis=1)).astype(jnp.bfloat16)
    seq_weight = jnp.einsum('ts,tq->sq', combine.astype(jnp.float32), pool, precision=lax.Precision.HIGHEST)
    return (pool, dispatch, combine, seq_weight)

def reference(hidden, w_gate, w_up, w_down, expert_ids, route_weight, seq_len, positive):
    high = lax.Precision.HIGHEST
    gate_f = w_gate.astype(jnp.float32)
    up_f = w_up.astype(jnp.float32)
    down_f = w_down.astype(jnp.float32)
    rows_hid = hidden.reshape(N_DP, N_EXPERT, TOK_DEV, D)
    rows_ids = expert_ids.reshape(N_DP, N_EXPERT, TOK_DEV, TOP)
    rows_gts = route_weight.reshape(N_DP, N_EXPERT, TOK_DEV, TOP)
    rows_len = seq_len.reshape(N_DP, N_EXPERT, SEQ_DEV)

    def tables(ids, gts, lens):
        return slot_tables(ids, gts, lens, EXPERTS, CAP)

    def expert_front(hid, ids, gts, lens):
        pool, dispatch, combine, seq_weight = jax.vmap(tables)(ids, gts, lens)
        slots = rounded(jnp.einsum('jts,jtd->jsd', dispatch.astype(jnp.float32), hid.astype(jnp.float32), precision=high))
        slots = slots.reshape(N_EXPERT, EXPERTS, CAP, D)
        gate_pre = jnp.einsum('jecd,edf->jecf', slots, gate_f, precision=high)
        up_pre = jnp.einsum('jecd,edf->jecf', slots, up_f, precision=high)
        act, slope = silu_parts(gate_pre)
        inner = rounded(act * up_pre)
        return (pool, combine, seq_weight, slots, up_pre, act, slope, inner)

    def forward_row(row):
        hid, ids, gts, lens = row
        pool, combine, seq_weight, slots, up_pre, act, slope, inner = expert_front(hid, ids, gts, lens)
        out_rows = rounded(jnp.einsum('jecf,efd->jecd', inner, down_f, precision=high))
        out_rows = out_rows.reshape(N_EXPERT, EXPERTS * CAP, D)
        mixed = hid.astype(jnp.float32) + jnp.einsum('jts,jsd->jtd', combine.astype(jnp.float32), out_rows, precision=high)
        return jnp.einsum('jtq,jtd->jqd', pool, mixed, precision=high)
    pooled = lax.map(forward_row, (rows_hid, rows_ids, rows_gts, rows_len))
    scale = lax.rsqrt(lax.optimization_barrier(jnp.sum(pooled * pooled, axis=-1)) + norm_eps)
    embed = rounded(pooled * scale[..., None])
    queries = embed[:, :, :QRY_DEV]
    passages = embed[:, :, QRY_DEV:]
    negatives = jnp.transpose(passages, (1, 0, 2, 3)).reshape(N_EXPERT, N_DP * PSG_DEV, D)
    scores = jnp.einsum('ijqd,jpd->ijqp', queries, negatives, precision=high) * inv_temp
    total = jnp.log(lax.optimization_barrier(jnp.sum(jnp.exp(scores), axis=-1)))
    pos = positive.reshape(N_DP, N_EXPERT, QRY_DEV)
    target = jnp.arange(N_DP * PSG_DEV, dtype=jnp.int32)[None, None, None, :] == pos[..., None]
    loss = total - lax.optimization_barrier(jnp.sum(jnp.where(target, scores, 0.0), axis=-1))
    coeff = (jnp.exp(scores - total[..., None]) - target.astype(jnp.float32)) * (loss_scale * inv_temp)
    grad_q = jnp.einsum('ijqp,jpd->ijqd', coeff, negatives, precision=high)
    grad_n = jnp.einsum('ijqp,ijqd->jpd', coeff, queries, precision=high)
    grad_p = jnp.transpose(grad_n.reshape(N_EXPERT, N_DP, PSG_DEV, D), (1, 0, 2, 3))
    grad_e = jnp.concatenate([grad_q, grad_p], axis=2)
    along = lax.optimization_barrier(jnp.sum(pooled * grad_e, axis=-1))
    grad_v = scale[..., None] * grad_e - pooled * (scale * scale * scale * along)[..., None]

    def backward_row(carry, row):
        hid, ids, gts, lens, gv = row
        pool, combine, seq_weight, slots, up_pre, act, slope, inner = expert_front(hid, ids, gts, lens)
        grad_rows = rounded(jnp.einsum('jsq,jqd->jsd', seq_weight, gv, precision=high)).reshape(N_EXPERT, EXPERTS, CAP, D)
        part_down = jnp.einsum('jecf,jecd->efd', inner, grad_rows, precision=high)
        grad_inner = jnp.einsum('jecd,efd->jecf', grad_rows, down_f, precision=high)
        grad_gate_pre = rounded(grad_inner * up_pre * slope)
        grad_up_pre = rounded(grad_inner * act)
        part_gate = jnp.einsum('jecd,jecf->edf', slots, grad_gate_pre, precision=high)
        part_up = jnp.einsum('jecd,jecf->edf', slots, grad_up_pre, precision=high)
        return ((carry[0] + rounded(part_gate), carry[1] + rounded(part_up), carry[2] + rounded(part_down)), None)
    start = (jnp.zeros((EXPERTS, D, FF), jnp.float32), jnp.zeros((EXPERTS, D, FF), jnp.float32), jnp.zeros((EXPERTS, FF, D), jnp.float32))
    grads, unused = lax.scan(backward_row, start, (rows_hid, rows_ids, rows_gts, rows_len, grad_v))
    return (loss.reshape(QUERIES), grads[0], grads[1], grads[2])
```

```python
import functools

import jax
import jax.numpy as jnp
from jax import lax
from jax.experimental import pallas as pl
from jax.experimental.pallas import tpu as pltpu
from jax.sharding import Mesh
from jax.sharding import PartitionSpec as P

inv_temp = 20.0
loss_scale = 128.0
norm_eps = 1e-06

BF = jnp.bfloat16
F32 = jnp.float32
I32 = jnp.int32

PART = 80
WIN = 48
SHIFT = 32
META = 44
SEQ_PAD = 4

NN = (((1,), (0,)), ((), ()))
NT = (((1,), (1,)), ((), ()))
TN = (((0,), (0,)), ((), ()))


def iota(shape, axis):
    return lax.broadcasted_iota(I32, shape, axis)


def mm(a, b, dims=NN):
    return lax.dot_general(a, b, dims, preferred_element_type=F32)


def split2(value):
    high = value.astype(BF)
    return high, (value - high.astype(F32)).astype(BF)


def split3(value):
    high = value.astype(BF)
    rest = value - high.astype(F32)
    mid = rest.astype(BF)
    return high, mid, (rest - mid.astype(F32)).astype(BF)


def window_row(expert, place):
    odd = (expert & 1) == 1
    return jnp.where(odd, jnp.where(place < 32, place + 16, place - 26), place)


def dispatch_kernel(length, rows_step, len_ref, ids_ref, rw_ref, hid_ref, out_ref, sum_ref, slot_ref, meta_ref):
    top, tok = ids_ref.shape
    experts = meta_ref.shape[0] // 2
    step = pl.program_id(0)

    @pl.when(step == 0)
    def _():
        pos = iota((1, tok), 1)
        seq = jnp.zeros((1, tok), I32)
        bound = jnp.full((1, tok), len_ref[0], I32)
        for s in range(1, len_ref.shape[0]):
            later = pos >= s * length
            seq = seq + later.astype(I32)
            bound = jnp.where(later, len_ref[s], bound)
        valid = pos - seq * length < bound
        ids = jnp.where(valid, ids_ref[...], -1)
        names = iota((experts, tok), 0)
        hits = [(ids[k : k + 1] == names).astype(F32) for k in range(top)]
        count = functools.reduce(jnp.add, hits)
        earlier = (iota((tok, tok), 0) < iota((tok, tok), 1)).astype(BF)
        before = mm(count.astype(BF), earlier)
        weight = rw_ref[...].astype(F32)
        lane = iota((128, tok), 0)
        marks = (seq + 1).astype(F32)
        meta = jnp.zeros((2 * experts, 128), F32)
        for k in range(top):
            place = jnp.sum(hits[k] * before, axis=0, keepdims=True).astype(I32)
            for m in range(k):
                place = place + (ids[m : m + 1] == ids[k : k + 1]).astype(I32)
            expert = ids[k : k + 1]
            spot = window_row(expert, place)
            where = (expert >> 1) * PART + (expert & 1) * SHIFT + spot
            slot_ref[k : k + 1, :] = jnp.where(valid, where, -1)
            chosen = (lane == spot).astype(BF)
            both = jnp.concatenate([hits[k] * weight[k : k + 1], hits[k] * marks], axis=0)
            meta = meta + mm(both.astype(BF), chosen, NT)
        meta_ref[...] = meta.astype(BF)
        member = jnp.logical_and(iota((8, tok), 0) == seq, valid).astype(BF)
        sum_ref[...] = mm(member, hid_ref[...])

    row = iota((rows_step, tok), 0) + step * rows_step
    picked = row == slot_ref[0:1, :]
    for k in range(1, top):
        picked = jnp.logical_or(picked, row == slot_ref[k : k + 1, :])
    out = mm(picked.astype(BF), hid_ref[...])
    line = iota((rows_step, 2 * experts), 0) + step * rows_step
    col = iota((rows_step, 2 * experts), 1)
    mark = (col >= experts).astype(I32)
    expert = col - experts * mark
    target = (expert >> 1) * PART + META + 2 * (expert & 1) + mark
    extra = mm((line == target).astype(BF), meta_ref[...])
    out_ref[:, 128:] = out[:, 128:].astype(BF)
    out_ref[:, :128] = (out[:, :128] + extra).astype(BF)


def forward_kernel(groups, seqs, arr_ref, gate_ref, up_ref, down_ref, part_ref, a_ref, keep_ref, w_ref, acc_ref):
    width = arr_ref.shape[2]
    e = pl.program_id(0)
    rows = groups * WIN
    quads = groups * SEQ_PAD

    def run(h):
        x = arr_ref[:, h * SHIFT : h * SHIFT + WIN, :].reshape(rows, width)
        gate = mm(x, gate_ref[0])
        up = mm(x, up_ref[0])
        sigma = jax.nn.sigmoid(gate)
        act = gate * sigma
        slope = sigma * (1.0 + gate * (1.0 - sigma))
        ff = gate.shape[1]
        keep_ref[0, :, 0:ff] = (up * slope).astype(BF)
        keep_ref[0, :, ff : 2 * ff] = act.astype(BF)
        inner = (act * up).astype(BF)
        tail = arr_ref[:, 32:48, 0:128].astype(F32)
        at = META - 32 + 2 * h
        wrow = tail[:, at, :].astype(BF)
        srow = tail[:, at + 1, :].astype(BF)
        owner = (iota((quads, groups), 0) >> 2 == iota((quads, groups), 1)).astype(BF)
        wrep = mm(owner, wrow)
        srep = mm(owner, srow)
        number = ((iota((quads, 128), 0) & 3) + 1).astype(F32)
        picked = jnp.where(srep == number, wrep, 0.0).astype(BF)
        spread = jnp.zeros((128, rows), jnp.bool_)
        line, col = iota((128, rows), 0), iota((128, rows), 1)
        for g in range(groups):
            spread = jnp.logical_or(spread, col == line + g * WIN)
        spread = jnp.logical_and(spread, line < WIN).astype(BF)
        block = iota((quads, rows), 0) >> 2
        start = block * WIN
        col = iota((quads, rows), 1)
        inside = jnp.logical_and(col >= start, col < start + WIN)
        weights = jnp.where(inside, mm(picked, spread), 0.0).astype(BF)
        w_ref[0] = weights
        a = mm(weights, inner)
        high, low = split2(a)
        a_ref[...] = high
        both = mm(jnp.concatenate([high, low], axis=0), down_ref[0])
        total = both[:quads] + both[quads:]
        if h == 0:
            acc_ref[...] = total
        else:
            total = total + acc_ref[...]
            for g in range(groups):
                part_ref[g] = total[g * SEQ_PAD : g * SEQ_PAD + SEQ_PAD]

    @pl.when(e == 0)
    def _():
        run(0)

    @pl.when(e == 1)
    def _():
        run(1)


def pool_kernel(len_ref, pos_ref, recv_ref, sum_ref, out_ref):
    groups = recv_ref.shape[0]
    width = recv_ref.shape[2]
    total = sum_ref[0:SEQ_PAD, :]
    for g in range(groups):
        total = total + recv_ref[g]
    row, col = iota((SEQ_PAD, width), 0), iota((SEQ_PAD, width), 1)
    inverse = jnp.zeros((SEQ_PAD, width), F32)
    count = len_ref.shape[0]
    positive = pos_ref[0]
    target = (positive >> 1) * SEQ_PAD + 1 + (positive & 1)
    note = jnp.where(col == 0, target, 0)
    for s in range(count):
        inverse = jnp.where(row == s, 1.0 / jnp.full((SEQ_PAD, width), len_ref[s], I32).astype(F32), inverse)
        note = jnp.where(col == 1 + s, len_ref[s], note)
    value = jnp.where(row == count, note.astype(F32), total * inverse)
    for g in range(groups):
        out_ref[g] = value


def contrast_kernel(at_ref, recv_ref, loss_ref, own_ref, slice_ref, all_ref, grad_ref):
    groups = recv_ref.shape[0]
    width = recv_ref.shape[2]
    quads = groups * SEQ_PAD
    me = at_ref[0]
    for g in range(groups):
        all_ref[g * SEQ_PAD : (g + 1) * SEQ_PAD, :] = recv_ref[g]
    raw = all_ref[...]
    row = iota((quads, 1), 0)
    kind = row & 3
    pooled = jnp.where(kind == 3, 0.0, raw)
    scale = lax.rsqrt(jnp.sum(pooled * pooled, axis=1, keepdims=True) + norm_eps)
    embed = (pooled * scale).astype(BF)
    notes = raw[:, 0:128].astype(BF)
    shift = (iota((quads, quads), 1) == (iota((quads, quads), 0) | 3)).astype(BF)
    notes = mm(shift, jnp.where(iota((quads, 128), 0) & 3 == 3, notes.astype(F32), 0.0).astype(BF))
    lane = iota((quads, 128), 1)
    target = jnp.sum(jnp.where(lane == 0, notes, 0.0), axis=1, keepdims=True)
    length = jnp.sum(jnp.where(lane == 1 + (iota((quads, 128), 0) & 3), notes, 0.0), axis=1, keepdims=True)
    inverse = jnp.where(kind == 3, 0.0, 1.0 / jnp.where(kind == 3, 1.0, length))
    scores = mm(embed, embed, NT) * inv_temp
    col = iota((quads, quads), 1)
    passage = jnp.logical_or((col & 3) == 1, (col & 3) == 2)
    total = jnp.log(jnp.sum(jnp.where(passage, jnp.exp(scores), 0.0), axis=1, keepdims=True))
    hit = (col.astype(F32) == target).astype(F32)
    losses = total - jnp.sum(hit * scores, axis=1, keepdims=True)
    wanted = iota((quads, 128), 0) == me * SEQ_PAD
    loss_ref[...] = jnp.sum(jnp.where(wanted, losses, 0.0), axis=0, keepdims=True)
    coeff = (jnp.where(passage, jnp.exp(scores - total), 0.0) - hit) * (loss_scale * inv_temp)
    coeff = jnp.where(iota((quads, quads), 0) & 3 == 0, coeff, 0.0)
    coeff = coeff + coeff.T
    three = mm(jnp.concatenate(split3(coeff), axis=0), embed)
    grad = three[:quads] + three[quads : 2 * quads] + three[2 * quads :]
    along = jnp.sum(pooled * grad, axis=1, keepdims=True)
    grad = scale * grad - pooled * (scale * scale * scale * along)
    grad = grad * inverse
    for g in range(groups):
        grad_ref[g] = grad[g * SEQ_PAD : (g + 1) * SEQ_PAD]
    own_ref[...] = grad_ref[me]
    slice_ref[...] = grad_ref[:, :, pl.ds(pl.multiple_of(me * 128, 128), 128)]


def backward_kernel(groups, cols, grad_ref, keep_ref, w_ref, down_ref, arr_ref, out_ref, pre_ref):
    local = keep_ref.shape[0]
    rows = groups * WIN
    ff = down_ref.shape[1]

    @pl.when(pl.program_id(0) == 0)
    def _():
        grad = grad_ref[...]
        for e in range(local):
            back = mm(grad, down_ref[e], NT)
            high, low = split2(back)
            two = jnp.concatenate([high, low], axis=0)
            weights = w_ref[e]
            inner = mm(jnp.concatenate([weights, weights], axis=0), two, TN)
            pre_ref[e, :, 0:ff] = (inner * keep_ref[e, :, 0:ff].astype(F32)).astype(BF)
            pre_ref[e, :, ff : 2 * ff] = (inner * keep_ref[e, :, ff : 2 * ff].astype(F32)).astype(BF)

    for e in range(local):
        x = arr_ref[:, e * SHIFT : e * SHIFT + WIN, :].reshape(rows, cols)
        part = mm(x, pre_ref[e], TN).astype(BF)
        for c in range(cols // 128):
            out_ref[c, e] = part[c * 128 : (c + 1) * 128]


def body(hidden, w_gate, w_up, w_down, expert_ids, route_weight, seq_len, positive):
    dp, ep = ("z", "core"), ("x", "y")
    tok, width = hidden.shape
    local, _, ff = w_gate.shape
    groups = lax.axis_size(ep)
    members = lax.axis_size(dp)
    experts = local * groups
    seqs = seq_len.shape[0]
    top = expert_ids.shape[1]
    length = tok // seqs
    quads = groups * SEQ_PAD
    rows = groups * WIN
    me = lax.axis_index(dp).astype(I32).reshape(1)
    smem = pl.BlockSpec(memory_space=pltpu.SMEM)
    big = pltpu.CompilerParams(vmem_limit_bytes=50 * 1024 * 1024)

    steps = 8
    rows_step = groups * PART // steps
    outgoing, hidden_sum = pl.pallas_call(
        functools.partial(dispatch_kernel, length, rows_step),
        grid=(steps,),
        out_shape=(
            jax.ShapeDtypeStruct((groups * PART, width), BF),
            jax.ShapeDtypeStruct((8, width), F32),
        ),
        in_specs=[
            smem,
            pl.BlockSpec((top, tok), lambda i: (0, 0)),
            pl.BlockSpec((top, tok), lambda i: (0, 0)),
            pl.BlockSpec((tok, width), lambda i: (0, 0)),
        ],
        out_specs=(
            pl.BlockSpec((rows_step, width), lambda i: (i, 0)),
            pl.BlockSpec((8, width), lambda i: (0, 0)),
        ),
        scratch_shapes=[pltpu.VMEM((top, tok), I32), pltpu.VMEM((2 * experts, 128), BF)],
        compiler_params=big,
        name="dispatch",
    )(seq_len, expert_ids.T, route_weight.T, hidden)

    arrived = lax.all_to_all(
        outgoing.reshape(groups, PART, width), ep, split_axis=0, concat_axis=0, tiled=True
    )

    partial, summed, keep, weights = pl.pallas_call(
        functools.partial(forward_kernel, groups, seqs),
        grid=(local,),
        out_shape=(
            jax.ShapeDtypeStruct((groups, SEQ_PAD, width), F32),
            jax.ShapeDtypeStruct((quads, local * ff), BF),
            jax.ShapeDtypeStruct((local, rows, 2 * ff), BF),
            jax.ShapeDtypeStruct((local, quads, rows), BF),
        ),
        in_specs=[
            pl.BlockSpec((groups, PART, width), lambda e: (0, 0, 0)),
            pl.BlockSpec((1, width, ff), lambda e: (e, 0, 0)),
            pl.BlockSpec((1, width, ff), lambda e: (e, 0, 0)),
            pl.BlockSpec((1, ff, width), lambda e: (e, 0, 0)),
        ],
        out_specs=(
            pl.BlockSpec((groups, SEQ_PAD, width), lambda e: (0, 0, 0)),
            pl.BlockSpec((quads, ff), lambda e: (0, e)),
            pl.BlockSpec((1, rows, 2 * ff), lambda e: (e, 0, 0)),
            pl.BlockSpec((1, quads, rows), lambda e: (e, 0, 0)),
        ),
        scratch_shapes=[pltpu.VMEM((quads, width), F32)],
        compiler_params=big,
        name="forward",
    )(arrived, w_gate, w_up, w_down)

    all_summed = lax.all_gather(summed, dp, axis=0, tiled=True)
    returned = lax.all_to_all(partial, ep, split_axis=0, concat_axis=0, tiled=True)

    vmem = pl.BlockSpec(memory_space=pltpu.VMEM)
    pooled = pl.pallas_call(
        pool_kernel,
        out_shape=jax.ShapeDtypeStruct((members, SEQ_PAD, width), F32),
        in_specs=[smem, smem, vmem, vmem],
        out_specs=vmem,
        compiler_params=big,
        name="pool",
    )(seq_len, positive, returned, hidden_sum)
    column = lax.all_to_all(pooled, dp, split_axis=0, concat_axis=0, tiled=True)

    loss, own, slices = pl.pallas_call(
        contrast_kernel,
        out_shape=(
            jax.ShapeDtypeStruct((1, 128), F32),
            jax.ShapeDtypeStruct((SEQ_PAD, width), F32),
            jax.ShapeDtypeStruct((members, SEQ_PAD, 128), F32),
        ),
        in_specs=[smem, vmem],
        out_specs=(vmem, vmem, vmem),
        scratch_shapes=[
            pltpu.VMEM((members * SEQ_PAD, width), F32),
            pltpu.VMEM((members, SEQ_PAD, width), F32),
        ],
        compiler_params=big,
        name="contrast",
    )(me, column)
    note = jnp.concatenate(
        [own.astype(BF).reshape(-1, 128), slices.astype(BF).reshape(-1, 128)], axis=0
    )
    spread = lax.all_to_all(
        jnp.broadcast_to(note[None], (groups,) + note.shape), ep, split_axis=0, concat_axis=0, tiled=True
    )
    half = SEQ_PAD * width // 128
    grads = spread[:, :half].reshape(quads, width)
    columns = spread[:, half:].reshape(groups, members, SEQ_PAD, 128)
    columns = jnp.transpose(columns, (1, 0, 2, 3)).reshape(members * quads, 128)

    cols = 256
    shards = width // 128
    partials = pl.pallas_call(
        functools.partial(backward_kernel, groups, cols),
        grid=(width // cols,),
        out_shape=jax.ShapeDtypeStruct((shards, local, 128, 2 * ff), BF),
        in_specs=[
            pl.BlockSpec((quads, width), lambda i: (0, 0)),
            pl.BlockSpec((local, rows, 2 * ff), lambda i: (0, 0, 0)),
            pl.BlockSpec((local, quads, rows), lambda i: (0, 0, 0)),
            pl.BlockSpec((local, ff, width), lambda i: (0, 0, 0)),
            pl.BlockSpec((groups, PART, cols), lambda i: (0, 0, i)),
        ],
        out_specs=pl.BlockSpec((cols // 128, local, 128, 2 * ff), lambda i: (i, 0, 0, 0)),
        scratch_shapes=[pltpu.VMEM((local, rows, 2 * ff), BF)],
        compiler_params=big,
        name="backward",
    )(grads, keep, weights, w_down, arrived)
    reduced = lax.psum_scatter(
        partials.reshape(shards * local * 128, 2 * ff), dp, scatter_dimension=0, tiled=True
    ).reshape(local, 128, 2 * ff)
    grad_down = jnp.einsum(
        "qef,qd->efd",
        all_summed.reshape(members * quads, local, ff),
        columns,
        preferred_element_type=F32,
    )
    return (
        loss[0, :1],
        reduced[:, :, :ff].astype(F32),
        reduced[:, :, ff:].astype(F32),
        grad_down,
    )


def solution(mesh):
    mesh = Mesh(mesh.devices.reshape(8, 2, 4, 4), ("z", "core", "x", "y"))
    dp, ep = ("z", "core"), ("x", "y")
    tokens = P(dp + ep)
    placed = (
        P(dp + ep, None),
        P(ep, None, None),
        P(ep, None, None),
        P(ep, None, None),
        P(dp + ep, None),
        P(dp + ep, None),
        tokens,
        tokens,
    )
    return jax.shard_map(
        body,
        mesh=mesh,
        in_specs=placed,
        out_specs=(tokens, P(ep, dp, None), P(ep, dp, None), P(ep, None, dp)),
        check_vma=False,
    )
```

```python
import functools

import jax
import jax.numpy as jnp
from jax import lax
from jax.experimental import pallas as pl
from jax.experimental.pallas import tpu as pltpu
from jax.sharding import Mesh
from jax.sharding import PartitionSpec as P

inv_temp = 20.0
loss_scale = 128.0
norm_eps = 1e-06

BF = jnp.bfloat16
F32 = jnp.float32
I32 = jnp.int32

PART = 80
WIN = 48
SHIFT = 32
META = 44
SEQS = 3
EXPERTS = 32
LINE = 4
NOTE = 16

NN = (((1,), (0,)), ((), ()))
NT = (((1,), (1,)), ((), ()))
TN = (((0,), (0,)), ((), ()))


def iota(shape, axis):
    return lax.broadcasted_iota(I32, shape, axis)


def mm(a, b, dims=NN):
    return lax.dot_general(a, b, dims, preferred_element_type=F32)


def split2(value):
    high = value.astype(BF)
    return high, (value - high.astype(F32)).astype(BF)


def split3(value):
    high = value.astype(BF)
    rest = value - high.astype(F32)
    mid = rest.astype(BF)
    return high, mid, (rest - mid.astype(F32)).astype(BF)


def third(row):
    return (row * 43) >> 7


def window_row(expert, place):
    odd = (expert & 1) == 1
    return jnp.where(odd, jnp.where(place < 32, place + 16, place - 26), place)


def prepare_kernel(length, len_ref, ids_ref, rw_ref, hid_ref, out_ref, sum_ref):
    top, tok = ids_ref.shape
    experts = EXPERTS
    pos = iota((1, tok), 1)
    seq = jnp.zeros((1, tok), I32)
    bound = jnp.full((1, tok), len_ref[0], I32)
    for s in range(1, len_ref.shape[0]):
        later = pos >= s * length
        seq = seq + later.astype(I32)
        bound = jnp.where(later, len_ref[s], bound)
    valid = pos - seq * length < bound
    ids = jnp.where(valid, ids_ref[...], -1)
    names = iota((experts, tok), 0)
    hits = [(ids[k : k + 1] == names).astype(F32) for k in range(top)]
    count = functools.reduce(jnp.add, hits)
    earlier = (iota((tok, tok), 0) < iota((tok, tok), 1)).astype(BF)
    before = mm(count.astype(BF), earlier)
    weight = rw_ref[...].astype(F32)
    lane = iota((128, tok), 0)
    marks = (seq + 1).astype(F32)
    meta = jnp.zeros((2 * experts, 128), F32)
    spots = []
    for k in range(top):
        place = jnp.sum(hits[k] * before, axis=0, keepdims=True).astype(I32)
        for m in range(k):
            place = place + (ids[m : m + 1] == ids[k : k + 1]).astype(I32)
        spot = window_row(ids[k : k + 1], place)
        spots.append(spot)
        chosen = (lane == spot).astype(BF)
        both = jnp.concatenate([hits[k] * weight[k : k + 1], hits[k] * marks], axis=0)
        meta = meta + mm(both.astype(BF), chosen, NT)
    meta = meta.astype(BF)
    member = jnp.logical_and(iota((8, tok), 0) == seq, valid).astype(BF)
    sum_ref[...] = mm(member, hid_ref[...])
    note = jnp.concatenate([ids.astype(F32), jnp.concatenate(spots, axis=0).astype(F32)], axis=0).astype(BF)
    out_ref[:tok, :] = hid_ref[...]
    out_ref[tok:, :] = jnp.zeros((NOTE, hid_ref.shape[1]), BF)
    out_ref[tok:, 0:tok] = note
    for c in range(2 * experts // NOTE):
        out_ref[tok:, 256 + c * 128 : 384 + c * 128] = meta[c * NOTE : (c + 1) * NOTE]


def select_kernel(at_ref, *refs):
    inputs, outputs = refs[:LINE], refs[LINE:]
    tok = inputs[0].shape[0] - NOTE
    x, y, core = at_ref[0], at_ref[1], at_ref[2]
    m = pl.program_id(0)
    for source in range(LINE):
        message = inputs[source]

        @pl.when(m == source)
        def _(message=message):
            note = message[tok:, 0:tok].astype(F32)
            ids = note[0 : NOTE // 2].astype(I32)
            spots = note[NOTE // 2 :].astype(I32)
            device = ids >> 1
            row = (ids & 1) * SHIFT + spots
            line = iota((PART, tok), 0)
            meta = jnp.concatenate(
                [message[tok:, 256 + c * 128 : 384 + c * 128] for c in range(2 * EXPERTS // NOTE)], axis=0
            )
            rows = iota((PART, 2 * EXPERTS), 0)
            col = iota((PART, 2 * EXPERTS), 1)
            mark = (col >= EXPERTS).astype(I32)
            expert = col - EXPERTS * mark
            noted = rows == META + 2 * (expert & 1) + mark
            wanted = []
            chosen = []
            for k in range(LINE):
                j = jnp.where(
                    core == 0,
                    x * LINE + ((y + k) & (LINE - 1)),
                    ((x + k) & (LINE - 1)) * LINE + y,
                )
                spot = jnp.where(device == j, row, -1)
                picked = line == spot[0:1]
                for t in range(1, NOTE // 2):
                    picked = jnp.logical_or(picked, line == spot[t : t + 1])
                wanted.append(picked.astype(BF))
                chosen.append(jnp.logical_and(noted, expert >> 1 == j).astype(BF))
            out = mm(jnp.concatenate(wanted, axis=0), message[:tok, :])
            extra = mm(jnp.concatenate(chosen, axis=0), meta)
            for k in range(LINE):
                part = slice(k * PART, (k + 1) * PART)
                outputs[k][0, :, 128:] = out[part, 128:].astype(BF)
                outputs[k][0, :, :128] = (out[part, :128] + extra[part]).astype(BF)


def forward_kernel(groups, at_ref, *refs):
    arrived = refs[:LINE]
    gate_ref, up_ref, down_ref, part_ref, a_ref, keep_ref, w_ref, x_ref, acc_ref = refs[LINE:]
    e = pl.program_id(0)
    here_x, here_y, core = at_ref[0], at_ref[1], at_ref[2]
    rows = groups * WIN
    owned = groups * SEQS
    chunks = x_ref.shape[2] // 128

    def run(h):
        window = slice(h * SHIFT, h * SHIFT + WIN)
        for r in range(groups):
            x_ref[0, r * WIN : (r + 1) * WIN, :] = arrived[r % LINE][r // LINE, window, :]
        x = x_ref[0]
        gate = mm(x, gate_ref[0])
        up = mm(x, up_ref[0])
        sigma = jax.nn.sigmoid(gate)
        act = gate * sigma
        slope = sigma * (1.0 + gate * (1.0 - sigma))
        ff = gate.shape[1]
        keep_ref[0, :, 0:ff] = (up * slope).astype(BF)
        keep_ref[0, :, ff : 2 * ff] = act.astype(BF)
        inner = (act * up).astype(BF)
        at = META - 32 + 2 * h
        tails = [arrived[r % LINE][r // LINE, 32:48, 0:128].astype(F32) for r in range(groups)]
        wrow = jnp.concatenate([t[at : at + 1] for t in tails], axis=0).astype(BF)
        srow = jnp.concatenate([t[at + 1 : at + 2] for t in tails], axis=0).astype(BF)

        def relative(shape):
            block = third(iota(shape, 0))
            by_x = (here_x - (block >> 2)) & 3
            by_y = (here_y - (block & 3)) & 3
            return jnp.where(core == 0, by_x * LINE + by_y, by_y * LINE + by_x)

        owner = (relative((owned, groups)) == iota((owned, groups), 1)).astype(BF)
        wrep = mm(owner, wrow)
        srep = mm(owner, srow)
        row = iota((owned, 128), 0)
        number = (row - SEQS * third(row) + 1).astype(F32)
        picked = jnp.where(srep == number, wrep, 0.0).astype(BF)
        spread = jnp.zeros((128, rows), jnp.bool_)
        line, col = iota((128, rows), 0), iota((128, rows), 1)
        for g in range(groups):
            spread = jnp.logical_or(spread, col == line + g * WIN)
        spread = jnp.logical_and(spread, line < WIN).astype(BF)
        start = relative((owned, rows)) * WIN
        col = iota((owned, rows), 1)
        inside = jnp.logical_and(col >= start, col < start + WIN)
        weights = jnp.where(inside, mm(picked, spread), 0.0).astype(BF)
        w_ref[0] = weights
        a = mm(weights, inner)
        high, low = split2(a)
        a_ref[...] = high
        both = mm(jnp.concatenate([high, low], axis=0), down_ref[0])
        total = both[:owned] + both[owned:]
        if h == 0:
            acc_ref[...] = total
        else:
            total = total + acc_ref[...]
            for g in range(groups):
                for c in range(chunks):
                    part_ref[g, c * SEQS : (c + 1) * SEQS, :] = total[
                        g * SEQS : (g + 1) * SEQS, c * 128 : (c + 1) * 128
                    ]

    @pl.when(e == 0)
    def _():
        run(0)

    @pl.when(e == 1)
    def _():
        run(1)


def pool_kernel(len_ref, pos_ref, recv_ref, sum_ref, out_ref, note_ref):
    groups, packed, _ = recv_ref.shape
    chunks = packed // SEQS
    total = recv_ref[0]
    for g in range(1, groups):
        total = total + recv_ref[g]
    note_ref[0:packed, :] = total
    total = jnp.concatenate([note_ref[c * SEQS : (c + 1) * SEQS, :] for c in range(chunks)], axis=1)
    row = iota((SEQS, 1), 0)
    inverse = jnp.zeros((SEQS, 1), F32)
    for s in range(SEQS):
        inverse = jnp.where(row == s, 1.0 / jnp.full((SEQS, 1), len_ref[s], I32).astype(F32), inverse)
    pooled = (total + sum_ref[0:SEQS, :]) * inverse
    scale = lax.rsqrt(jnp.sum(pooled * pooled, axis=1, keepdims=True) + norm_eps)
    positive = pos_ref[0]
    col = iota((1, 128), 1)
    note = jnp.where(col == 0, (positive >> 1) * SEQS + 1 + (positive & 1), 0)
    for s in range(SEQS):
        note = jnp.where(col == 1 + s, len_ref[s], note)
    note = note.astype(F32)
    for place, piece in enumerate(split3(scale)):
        piece = piece.astype(F32)
        for s in range(SEQS):
            note = jnp.where(col == 4 * (place + 1) + 1 + s, piece[s : s + 1], note)
    embed = pooled * scale
    for c in range(chunks):
        note_ref[c * SEQS : (c + 1) * SEQS, :] = embed[:, c * 128 : (c + 1) * 128]
    note_ref[packed:, :] = jnp.where(iota((NOTE, 128), 0) == 0, note, 0.0)
    value = note_ref[...].astype(BF)
    for g in range(groups):
        out_ref[g] = value


def contrast_kernel(at_ref, recv_ref, loss_ref, out_ref, all_ref, grad_ref, note_ref):
    groups = recv_ref.shape[0]
    packed = recv_ref.shape[1] - NOTE
    chunks = packed // SEQS
    owned = groups * SEQS
    me = at_ref[0]
    notes = []
    for g in range(groups):
        value = recv_ref[g].astype(F32)
        notes.append(value[packed : packed + 1])
        for c in range(chunks):
            all_ref[g * SEQS : (g + 1) * SEQS, c * 128 : (c + 1) * 128] = value[c * SEQS : (c + 1) * SEQS]
    notes = jnp.concatenate(notes, axis=0).astype(BF)

    def sort(shape, axis):
        place = iota(shape, axis)
        return place - SEQS * third(place)

    owner = (third(iota((owned, groups), 0)) == iota((owned, groups), 1)).astype(BF)
    notes = mm(owner, notes)
    lane = iota((owned, 128), 1)
    sub = sort((owned, 128), 0)
    target = jnp.sum(jnp.where(lane == 0, notes, 0.0), axis=1, keepdims=True)
    length = jnp.sum(jnp.where(lane == 1 + sub, notes, 0.0), axis=1, keepdims=True)
    pieces = jnp.logical_and(lane > 4, lane < 16)
    scale = jnp.sum(jnp.where(jnp.logical_and(pieces, (lane & 3) == 1 + sub), notes, 0.0), axis=1, keepdims=True)
    wide = all_ref[...]
    embed = wide.astype(BF)
    scores = mm(embed, embed, NT) * inv_temp
    passage = sort((owned, owned), 1) > 0
    total = jnp.log(jnp.sum(jnp.where(passage, jnp.exp(scores), 0.0), axis=1, keepdims=True))
    hit = (iota((owned, owned), 1).astype(F32) == target).astype(F32)
    losses = total - jnp.sum(hit * scores, axis=1, keepdims=True)
    wanted = iota((owned, 128), 0) == me * SEQS
    loss_ref[...] = jnp.sum(jnp.where(wanted, losses, 0.0), axis=0, keepdims=True)
    coeff = (jnp.where(passage, jnp.exp(scores - total), 0.0) - hit) * (loss_scale * inv_temp)
    coeff = jnp.where(sort((owned, owned), 0) == 0, coeff, 0.0)
    coeff = coeff + coeff.T
    three = mm(jnp.concatenate(split3(coeff), axis=0), embed)
    grad = three[:owned] + three[owned : 2 * owned] + three[2 * owned :]
    along = jnp.sum(wide * grad, axis=1, keepdims=True)
    grad = (grad - wide * along) * (scale / length)
    all_ref[...] = grad
    for g in range(groups):
        grad_ref[g] = grad[g * SEQS : (g + 1) * SEQS]
    own = grad_ref[me]
    for c in range(chunks):
        note_ref[c * SEQS : (c + 1) * SEQS, :] = own[:, c * 128 : (c + 1) * 128]
    note_ref[packed:, :] = all_ref[:, pl.ds(pl.multiple_of(me * 128, 128), 128)]
    value = note_ref[...].astype(BF)
    for g in range(out_ref.shape[0]):
        out_ref[g] = value


def weight_parts(core, x_ref, pre_ref, mine_ref, other_ref):
    for e in range(pre_ref.shape[0]):
        part = mm(x_ref[e], pre_ref[e], TN)
        half = part.shape[0] // 2
        first, second = part[:half], part[half:]
        mine_ref[0, e] = jnp.where(core == 0, first, second).astype(BF)
        other_ref[0, e] = jnp.where(core == 0, second, first).astype(BF)


def first_kernel(at_ref, recv_ref, keep_ref, w_ref, down_ref, x_ref, pre_ref, mine_ref, other_ref, grad_ref):
    ff = down_ref.shape[1]
    chunks = grad_ref.shape[1] // 128
    for g in range(recv_ref.shape[0]):
        value = recv_ref[g].astype(F32)
        for c in range(chunks):
            grad_ref[g * SEQS : (g + 1) * SEQS, c * 128 : (c + 1) * 128] = value[c * SEQS : (c + 1) * SEQS]
    grad = grad_ref[...].astype(BF)
    for e in range(keep_ref.shape[0]):
        back = mm(grad, down_ref[e], NT)
        high, low = split2(back)
        two = jnp.concatenate([high, low], axis=0)
        weights = w_ref[e]
        inner = mm(jnp.concatenate([weights, weights], axis=0), two, TN)
        pre_ref[e, :, 0:ff] = (inner * keep_ref[e, :, 0:ff].astype(F32)).astype(BF)
        pre_ref[e, :, ff : 2 * ff] = (inner * keep_ref[e, :, ff : 2 * ff].astype(F32)).astype(BF)
    weight_parts(at_ref[2], x_ref, pre_ref, mine_ref, other_ref)


def more_kernel(at_ref, pre_ref, x_ref, mine_ref, other_ref):
    weight_parts(at_ref[2], x_ref, pre_ref, mine_ref, other_ref)


def body(hidden, w_gate, w_up, w_down, expert_ids, route_weight, seq_len, positive):
    dp, ep = ("z", "core"), ("x", "y")
    tok, width = hidden.shape
    local, _, ff = w_gate.shape
    groups = lax.axis_size(ep)
    members = lax.axis_size(dp)
    top = expert_ids.shape[1]
    length = tok // SEQS
    owned = groups * SEQS
    packed = SEQS * width // 128
    rows = groups * WIN
    me = lax.axis_index(dp).astype(I32).reshape(1)
    smem = pl.BlockSpec(memory_space=pltpu.SMEM)
    big = pltpu.CompilerParams(vmem_limit_bytes=50 * 1024 * 1024)

    at = jnp.stack([lax.axis_index(a) for a in ("x", "y", "core", "z")]).astype(I32)
    vmem = pl.BlockSpec(memory_space=pltpu.VMEM)
    message, hidden_sum = pl.pallas_call(
        functools.partial(prepare_kernel, length),
        out_shape=(
            jax.ShapeDtypeStruct((tok + NOTE, width), BF),
            jax.ShapeDtypeStruct((8, width), F32),
        ),
        in_specs=[smem, vmem, vmem, vmem],
        out_specs=(vmem, vmem),
        name="prepare",
    )(seq_len, expert_ids.T, route_weight.T, hidden)

    def ahead(value, k, turned):
        pairs = []
        for core in range(2):
            for x in range(LINE):
                for y in range(LINE):
                    to = ((x + k) % LINE, y) if core == turned else (x, (y + k) % LINE)
                    pairs.append(((core * LINE + x) * LINE + y, (core * LINE + to[0]) * LINE + to[1]))
        return lax.ppermute(value, ("core", "x", "y"), pairs)

    gathered = {0: message}
    for k in (1, 3, 2):
        gathered[k] = ahead(message, k, 0)
    picked = pl.pallas_call(
        select_kernel,
        grid=(LINE,),
        out_shape=[jax.ShapeDtypeStruct((LINE, PART, width), BF)] * LINE,
        in_specs=[smem] + [pl.BlockSpec((tok + NOTE, width), lambda m: (0, 0))] * LINE,
        out_specs=[pl.BlockSpec((1, PART, width), lambda m: (m, 0, 0))] * LINE,
        compiler_params=big,
        name="select",
    )(at, *[gathered[k] for k in range(LINE)])
    arrived = {0: picked[0]}
    for k in (1, 3, 2):
        arrived[k] = ahead(picked[k], k, 1)

    partial, summed, keep, weights, rows_in = pl.pallas_call(
        functools.partial(forward_kernel, groups),
        grid=(local,),
        out_shape=(
            jax.ShapeDtypeStruct((groups, packed, 128), F32),
            jax.ShapeDtypeStruct((owned, local * ff), BF),
            jax.ShapeDtypeStruct((local, rows, 2 * ff), BF),
            jax.ShapeDtypeStruct((local, owned, rows), BF),
            jax.ShapeDtypeStruct((local, rows, width), BF),
        ),
        in_specs=[smem]
        + [pl.BlockSpec((LINE, PART, width), lambda e: (0, 0, 0))] * LINE
        + [
            pl.BlockSpec((1, width, ff), lambda e: (e, 0, 0)),
            pl.BlockSpec((1, width, ff), lambda e: (e, 0, 0)),
            pl.BlockSpec((1, ff, width), lambda e: (e, 0, 0)),
        ],
        out_specs=(
            pl.BlockSpec((groups, packed, 128), lambda e: (0, 0, 0)),
            pl.BlockSpec((owned, ff), lambda e: (0, e)),
            pl.BlockSpec((1, rows, 2 * ff), lambda e: (e, 0, 0)),
            pl.BlockSpec((1, owned, rows), lambda e: (e, 0, 0)),
            pl.BlockSpec((1, rows, width), lambda e: (e, 0, 0)),
        ),
        scratch_shapes=[pltpu.VMEM((owned, width), F32)],
        compiler_params=big,
        name="forward",
    )(at, *[arrived[k] for k in range(LINE)], w_gate, w_up, w_down)

    all_summed = lax.all_gather(summed, dp, axis=0, tiled=True)
    returned = lax.all_to_all(partial, ep, split_axis=0, concat_axis=0, tiled=True)

    pooled = pl.pallas_call(
        pool_kernel,
        out_shape=jax.ShapeDtypeStruct((members, packed + NOTE, 128), BF),
        in_specs=[smem, smem, vmem, vmem],
        out_specs=vmem,
        scratch_shapes=[pltpu.VMEM((packed + NOTE, 128), F32)],
        compiler_params=big,
        name="pool",
    )(seq_len, positive, returned, hidden_sum)
    column = lax.all_to_all(pooled, dp, split_axis=0, concat_axis=0, tiled=True)

    noted = packed + members * SEQS
    loss, note = pl.pallas_call(
        contrast_kernel,
        out_shape=(
            jax.ShapeDtypeStruct((1, 128), F32),
            jax.ShapeDtypeStruct((groups, noted, 128), BF),
        ),
        in_specs=[smem, vmem],
        out_specs=(vmem, vmem),
        scratch_shapes=[
            pltpu.VMEM((members * SEQS, width), F32),
            pltpu.VMEM((members, SEQS, width), F32),
            pltpu.VMEM((noted, 128), F32),
        ],
        compiler_params=big,
        name="contrast",
    )(me, column)
    spread = lax.all_to_all(note, ep, split_axis=0, concat_axis=0, tiled=True)
    columns = spread[:, packed:].reshape(groups, members, SEQS, 128)
    columns = jnp.transpose(columns, (1, 0, 2, 3)).reshape(members * owned, 128)

    ring = lax.axis_size("z")
    cols = width // ring
    piece = (local, cols // 2, 2 * ff)

    def shard_spec(order):
        return pl.BlockSpec((local, rows, cols), lambda i, at: (0, 0, (at[3] + order(i)) & (ring - 1)))

    def parts_spec():
        return pl.BlockSpec((1,) + piece, lambda i, at: (i, 0, 0, 0))

    def cost(shards, extra=0):
        flops = shards * local * 2 * rows * cols * 2 * ff
        return pl.CostEstimate(flops=flops, bytes_accessed=shards * 4 * local * rows * cols + extra, transcendentals=0)

    pre, mine, other = pl.pallas_call(
        first_kernel,
        grid_spec=pltpu.PrefetchScalarGridSpec(
            num_scalar_prefetch=1,
            grid=(1,),
            in_specs=[
                pl.BlockSpec((groups, noted, 128), lambda i, at: (0, 0, 0)),
                pl.BlockSpec((local, rows, 2 * ff), lambda i, at: (0, 0, 0)),
                pl.BlockSpec((local, owned, rows), lambda i, at: (0, 0, 0)),
                pl.BlockSpec((local, ff, width), lambda i, at: (0, 0, 0)),
                shard_spec(lambda i: 4),
            ],
            out_specs=[
                pl.BlockSpec((local, rows, 2 * ff), lambda i, at: (0, 0, 0)),
                parts_spec(),
                parts_spec(),
            ],
            scratch_shapes=[pltpu.VMEM((owned, width), F32)],
        ),
        out_shape=(
            jax.ShapeDtypeStruct((local, rows, 2 * ff), BF),
            jax.ShapeDtypeStruct((1,) + piece, BF),
            jax.ShapeDtypeStruct((1,) + piece, BF),
        ),
        cost_estimate=cost(1, 16 * 1024 * 1024),
        compiler_params=big,
        name="first_parts",
    )(at, spread, keep, weights, w_down, rows_in)

    def more(shards, order, name):
        return pl.pallas_call(
            more_kernel,
            grid_spec=pltpu.PrefetchScalarGridSpec(
                num_scalar_prefetch=1,
                grid=(shards,),
                in_specs=[
                    pl.BlockSpec((local, rows, 2 * ff), lambda i, at: (0, 0, 0)),
                    shard_spec(order),
                ],
                out_specs=[parts_spec(), parts_spec()],
            ),
            out_shape=[jax.ShapeDtypeStruct((shards,) + piece, BF)] * 2,
            cost_estimate=cost(shards),
            compiler_params=big,
            name=name,
        )(at, pre, rows_in)

    def swap(value):
        return lax.ppermute(value, "core", [(0, 1), (1, 0)])

    def along(value, k):
        return lax.ppermute(value, "z", [(i, (i + k) % ring) for i in range(ring)])

    def total(*values):
        return sum(v.astype(F32) for v in values)

    theirs = swap(other)
    held, sent = more(2, lambda i: 3 + 2 * i, "parts_three")
    up, down = total(mine[0, 0], theirs[0, 0]).astype(BF), total(mine[0, 1], theirs[0, 1]).astype(BF)
    up, down, pre, sent = lax.optimization_barrier((up, down, pre, sent))
    up, down, got = along(up, 1), along(down, -1), swap(sent)
    later = more(2, lambda i: 2 + 4 * i, "parts_two")
    up = jnp.stack([total(held[0, 0], got[0, 0], up), total(held[0, 1], got[0, 1])]).astype(BF)
    down = jnp.stack([total(held[1, 0], got[1, 0]), total(held[1, 1], got[1, 1], down)]).astype(BF)
    up, down, pre, later = lax.optimization_barrier((up, down, pre, later))
    held, sent = later
    up, down, got = along(up, 1), along(down, -1), swap(sent)
    later = more(3, lambda i: jnp.where(i == 0, 1, 7 * (2 - i)), "parts_one")
    up = total(held[0], got[0], up).astype(BF)
    down = total(held[1], got[1], down).astype(BF)
    up, down, later = lax.optimization_barrier((up, down, later))
    held, sent = later
    up, down, got = along(up, 1), along(down, -1), swap(sent)
    up = total(held[0], got[0], up).astype(BF)
    down = total(held[1], got[1], down).astype(BF)
    up, down = lax.optimization_barrier((up, down))
    up, down = along(up, 1), along(down, -1)
    reduced = total(held[2], got[2], up, down)
    grad_down = jnp.einsum(
        "qef,qd->efd",
        all_summed.reshape(members * owned, local, ff),
        columns,
        preferred_element_type=F32,
    )
    return (
        loss[0, :1],
        reduced[:, :, :ff],
        reduced[:, :, ff:],
        grad_down,
    )


def solution(mesh):
    mesh = Mesh(mesh.devices.reshape(8, 2, 4, 4), ("z", "core", "x", "y"))
    dp, ep = ("z", "core"), ("x", "y")
    tokens = P(dp + ep)
    placed = (
        P(dp + ep, None),
        P(ep, None, None),
        P(ep, None, None),
        P(ep, None, None),
        P(dp + ep, None),
        P(dp + ep, None),
        tokens,
        tokens,
    )
    return jax.shard_map(
        body,
        mesh=mesh,
        in_specs=placed,
        out_specs=(tokens, P(ep, dp, None), P(ep, dp, None), P(ep, None, dp)),
        check_vma=False,
    )
```

```python
import functools

import jax
import jax.numpy as jnp
from jax import lax
from jax.experimental import pallas as pl
from jax.experimental.pallas import tpu as pltpu
from jax.sharding import Mesh
from jax.sharding import PartitionSpec as P

inv_temp = 20.0
loss_scale = 128.0
norm_eps = 1e-06

BF = jnp.bfloat16
F32 = jnp.float32
I32 = jnp.int32

PART = 80
WIN = 48
SHIFT = 32
META = 44
SEQS = 3
EXPERTS = 32
LINE = 4
NOTE = 16

NN = (((1,), (0,)), ((), ()))
NT = (((1,), (1,)), ((), ()))
TN = (((0,), (0,)), ((), ()))


def iota(shape, axis):
    return lax.broadcasted_iota(I32, shape, axis)


def mm(a, b, dims=NN):
    return lax.dot_general(a, b, dims, preferred_element_type=F32)


def split2(value):
    high = value.astype(BF)
    return high, (value - high.astype(F32)).astype(BF)


def split3(value):
    high = value.astype(BF)
    rest = value - high.astype(F32)
    mid = rest.astype(BF)
    return high, mid, (rest - mid.astype(F32)).astype(BF)


def third(row):
    return (row * 43) >> 7


def window_row(expert, place):
    odd = (expert & 1) == 1
    return jnp.where(odd, jnp.where(place < 32, place + 16, place - 26), place)


def prepare_kernel(length, len_ref, ids_ref, rw_ref, hid_ref, out_ref, sum_ref):
    top, tok = ids_ref.shape
    experts = EXPERTS
    pos = iota((1, tok), 1)
    seq = jnp.zeros((1, tok), I32)
    bound = jnp.full((1, tok), len_ref[0], I32)
    for s in range(1, len_ref.shape[0]):
        later = pos >= s * length
        seq = seq + later.astype(I32)
        bound = jnp.where(later, len_ref[s], bound)
    valid = pos - seq * length < bound
    ids = jnp.where(valid, ids_ref[...], -1)
    names = iota((experts, tok), 0)
    hits = [(ids[k : k + 1] == names).astype(F32) for k in range(top)]
    count = functools.reduce(jnp.add, hits)
    earlier = (iota((tok, tok), 0) < iota((tok, tok), 1)).astype(BF)
    before = mm(count.astype(BF), earlier)
    weight = rw_ref[...].astype(F32)
    lane = iota((128, tok), 0)
    marks = (seq + 1).astype(F32)
    meta = jnp.zeros((2 * experts, 128), F32)
    spots = []
    for k in range(top):
        place = jnp.sum(hits[k] * before, axis=0, keepdims=True).astype(I32)
        for m in range(k):
            place = place + (ids[m : m + 1] == ids[k : k + 1]).astype(I32)
        spot = window_row(ids[k : k + 1], place)
        spots.append(spot)
        chosen = (lane == spot).astype(BF)
        both = jnp.concatenate([hits[k] * weight[k : k + 1], hits[k] * marks], axis=0)
        meta = meta + mm(both.astype(BF), chosen, NT)
    meta = meta.astype(BF)
    member = jnp.logical_and(iota((8, tok), 0) == seq, valid).astype(BF)
    sum_ref[...] = mm(member, hid_ref[...])
    note = jnp.concatenate([ids.astype(F32), jnp.concatenate(spots, axis=0).astype(F32)], axis=0).astype(BF)
    out_ref[:tok, :] = hid_ref[...]
    out_ref[tok:, :] = jnp.zeros((NOTE, hid_ref.shape[1]), BF)
    out_ref[tok:, 0:tok] = note
    for c in range(2 * experts // NOTE):
        out_ref[tok:, 256 + c * 128 : 384 + c * 128] = meta[c * NOTE : (c + 1) * NOTE]


def select_kernel(halves, at_ref, *refs):
    count = 1 if halves else 3
    inputs, outputs = refs[: 2 if halves else count], refs[2 if halves else count :]
    x, y, core = at_ref[0], at_ref[1], at_ref[2]
    m = pl.program_id(0)
    for source in range(count):

        @pl.when(m == source)
        def _(source=source):
            message = inputs[1] if halves else inputs[source]
            at = message.shape[0] - NOTE
            values = message[:at, :]
            if halves:
                values = jnp.concatenate([inputs[0][...], values], axis=0)
            tok = values.shape[0]
            note = message[at:, 0:tok].astype(F32)
            ids = note[0 : NOTE // 2].astype(I32)
            spots = note[NOTE // 2 :].astype(I32)
            device = ids >> 1
            row = (ids & 1) * SHIFT + spots
            line = iota((PART, tok), 0)
            meta = jnp.concatenate(
                [message[at:, 256 + c * 128 : 384 + c * 128] for c in range(2 * EXPERTS // NOTE)], axis=0
            )
            rows = iota((PART, 2 * EXPERTS), 0)
            col = iota((PART, 2 * EXPERTS), 1)
            mark = (col >= EXPERTS).astype(I32)
            expert = col - EXPERTS * mark
            noted = rows == META + 2 * (expert & 1) + mark
            wanted = []
            chosen = []
            for k in range(LINE):
                j = jnp.where(
                    core == 0,
                    x * LINE + ((y + k) & (LINE - 1)),
                    ((x + k) & (LINE - 1)) * LINE + y,
                )
                spot = jnp.where(device == j, row, -1)
                picked = line == spot[0:1]
                for t in range(1, NOTE // 2):
                    picked = jnp.logical_or(picked, line == spot[t : t + 1])
                wanted.append(picked.astype(BF))
                chosen.append(jnp.logical_and(noted, expert >> 1 == j).astype(BF))
            out = mm(jnp.concatenate(wanted, axis=0), values)
            extra = mm(jnp.concatenate(chosen, axis=0), meta)
            for k in range(LINE):
                part = slice(k * PART, (k + 1) * PART)
                ref = outputs[4 if k == 2 and source == 2 else k]
                ref[0, :, 128:] = out[part, 128:].astype(BF)
                ref[0, :, :128] = (out[part, :128] + extra[part]).astype(BF)


def window(ref, m, h, cols=slice(None)):
    return ref[m, h * SHIFT : h * SHIFT + WIN, cols]


def forward_kernel(layout, last, at_ref, *refs):
    arrays = max(spot[0] for spot in layout) + 1
    arrived = refs[:arrays]
    if last:
        gate_ref, up_ref, down_ref, before_ref, a_ref, keep_ref, w_ref, part_ref, acc_ref = refs[arrays:]
    else:
        gate_ref, up_ref, before_ref, a_ref, keep_ref, w_ref = refs[arrays:]
    e = pl.program_id(0)
    here_x, here_y, core = at_ref[0], at_ref[1], at_ref[2]
    blocks = len(layout)
    rows = blocks * WIN
    owned = before_ref.shape[0]
    groups = owned // SEQS

    def run(h):
        x = jnp.concatenate([window(arrived[n], i, h) for n, i, _, _ in layout], axis=0)
        gate = mm(x, gate_ref[0])
        up = mm(x, up_ref[0])
        sigma = jax.nn.sigmoid(gate)
        act = gate * sigma
        slope = sigma * (1.0 + gate * (1.0 - sigma))
        ff = gate.shape[1]
        keep_ref[0, :, 0:ff] = (up * slope).astype(BF)
        keep_ref[0, :, ff : 2 * ff] = act.astype(BF)
        inner = (act * up).astype(BF)
        at = META - 32 + 2 * h
        tails = [arrived[n][i, 32:48, 0:128].astype(F32) for n, i, _, _ in layout]
        pad = [jnp.zeros((8 - blocks, 128), F32)]
        wrow = jnp.concatenate([t[at : at + 1] for t in tails] + pad, axis=0).astype(BF)
        srow = jnp.concatenate([t[at + 1 : at + 2] for t in tails] + pad, axis=0).astype(BF)
        col8 = iota((owned, 8), 1)
        col = iota((owned, rows), 1)
        home8 = jnp.full((owned, 8), -1, I32)
        home = jnp.full((owned, rows), -1, I32)
        for r, (_, _, m, k) in enumerate(layout):
            first, second = (here_x - m) & 3, (here_y - k) & 3
            third_, fourth = (here_x - k) & 3, (here_y - m) & 3
            j = jnp.where(core == 0, first * LINE + second, third_ * LINE + fourth)
            home8 = jnp.where(col8 == r, j, home8)
            home = jnp.where(col >= r * WIN, j, home)
        owner = (third(iota((owned, 8), 0)) == home8).astype(BF)
        wrep = mm(owner, wrow)
        srep = mm(owner, srow)
        row = iota((owned, 128), 0)
        number = (row - SEQS * third(row) + 1).astype(F32)
        picked = jnp.where(srep == number, wrep, 0.0).astype(BF)
        place = iota((128, rows), 1)
        place = place - WIN * ((place * 683) >> 15)
        spread = (place == iota((128, rows), 0)).astype(BF)
        inside = third(iota((owned, rows), 0)) == home
        weights = jnp.where(inside, mm(picked, spread), 0.0).astype(BF)
        w_ref[0] = weights
        a = before_ref[...] + mm(weights, inner)
        if not last:
            a_ref[...] = a
            return
        high, low = split2(a)
        a_ref[...] = high
        both = mm(jnp.concatenate([high, low], axis=0), down_ref[0])
        total = both[:owned] + both[owned:]
        if h == 0:
            acc_ref[...] = total
        else:
            total = total + acc_ref[...]
            for g in range(groups):
                for c in range(total.shape[1] // 128):
                    part_ref[g, c * SEQS : (c + 1) * SEQS, :] = total[
                        g * SEQS : (g + 1) * SEQS, c * 128 : (c + 1) * 128
                    ]

    @pl.when(e == 0)
    def _():
        run(0)

    @pl.when(e == 1)
    def _():
        run(1)


def pool_kernel(len_ref, pos_ref, recv_ref, sum_ref, out_ref, note_ref):
    groups, packed, _ = recv_ref.shape
    chunks = packed // SEQS
    total = recv_ref[0]
    for g in range(1, groups):
        total = total + recv_ref[g]
    note_ref[0:packed, :] = total
    total = jnp.concatenate([note_ref[c * SEQS : (c + 1) * SEQS, :] for c in range(chunks)], axis=1)
    row = iota((SEQS, 1), 0)
    inverse = jnp.zeros((SEQS, 1), F32)
    for s in range(SEQS):
        inverse = jnp.where(row == s, 1.0 / jnp.full((SEQS, 1), len_ref[s], I32).astype(F32), inverse)
    pooled = (total + sum_ref[0:SEQS, :]) * inverse
    scale = lax.rsqrt(jnp.sum(pooled * pooled, axis=1, keepdims=True) + norm_eps)
    positive = pos_ref[0]
    col = iota((1, 128), 1)
    note = jnp.where(col == 0, (positive >> 1) * SEQS + 1 + (positive & 1), 0)
    for s in range(SEQS):
        note = jnp.where(col == 1 + s, len_ref[s], note)
    note = note.astype(F32)
    for place, piece in enumerate(split3(scale)):
        piece = piece.astype(F32)
        for s in range(SEQS):
            note = jnp.where(col == 4 * (place + 1) + 1 + s, piece[s : s + 1], note)
    embed = pooled * scale
    for c in range(chunks):
        note_ref[c * SEQS : (c + 1) * SEQS, :] = embed[:, c * 128 : (c + 1) * 128]
    note_ref[packed:, :] = jnp.where(iota((NOTE, 128), 0) == 0, note, 0.0)
    value = note_ref[...].astype(BF)
    for g in range(groups):
        out_ref[g] = value


def contrast_kernel(at_ref, recv_ref, loss_ref, out_ref, all_ref, grad_ref, note_ref):
    groups = recv_ref.shape[0]
    packed = recv_ref.shape[1] - NOTE
    chunks = packed // SEQS
    owned = groups * SEQS
    me = at_ref[0]
    notes = []
    for g in range(groups):
        value = recv_ref[g].astype(F32)
        notes.append(value[packed : packed + 1])
        for c in range(chunks):
            all_ref[g * SEQS : (g + 1) * SEQS, c * 128 : (c + 1) * 128] = value[c * SEQS : (c + 1) * SEQS]
    notes = jnp.concatenate(notes, axis=0).astype(BF)

    def sort(shape, axis):
        place = iota(shape, axis)
        return place - SEQS * third(place)

    owner = (third(iota((owned, groups), 0)) == iota((owned, groups), 1)).astype(BF)
    notes = mm(owner, notes)
    lane = iota((owned, 128), 1)
    sub = sort((owned, 128), 0)
    target = jnp.sum(jnp.where(lane == 0, notes, 0.0), axis=1, keepdims=True)
    length = jnp.sum(jnp.where(lane == 1 + sub, notes, 0.0), axis=1, keepdims=True)
    pieces = jnp.logical_and(lane > 4, lane < 16)
    scale = jnp.sum(jnp.where(jnp.logical_and(pieces, (lane & 3) == 1 + sub), notes, 0.0), axis=1, keepdims=True)
    wide = all_ref[...]
    embed = wide.astype(BF)
    scores = mm(embed, embed, NT) * inv_temp
    passage = sort((owned, owned), 1) > 0
    total = jnp.log(jnp.sum(jnp.where(passage, jnp.exp(scores), 0.0), axis=1, keepdims=True))
    hit = (iota((owned, owned), 1).astype(F32) == target).astype(F32)
    losses = total - jnp.sum(hit * scores, axis=1, keepdims=True)
    wanted = iota((owned, 128), 0) == me * SEQS
    loss_ref[...] = jnp.sum(jnp.where(wanted, losses, 0.0), axis=0, keepdims=True)
    coeff = (jnp.where(passage, jnp.exp(scores - total), 0.0) - hit) * (loss_scale * inv_temp)
    coeff = jnp.where(sort((owned, owned), 0) == 0, coeff, 0.0)
    coeff = coeff + coeff.T
    three = mm(jnp.concatenate(split3(coeff), axis=0), embed)
    grad = three[:owned] + three[owned : 2 * owned] + three[2 * owned :]
    along = jnp.sum(wide * grad, axis=1, keepdims=True)
    grad = (grad - wide * along) * (scale / length)
    all_ref[...] = grad
    for g in range(groups):
        grad_ref[g] = grad[g * SEQS : (g + 1) * SEQS]
    own = grad_ref[me]
    for c in range(chunks):
        note_ref[c * SEQS : (c + 1) * SEQS, :] = own[:, c * 128 : (c + 1) * 128]
    note_ref[packed:, :] = all_ref[:, pl.ds(pl.multiple_of(me * 128, 128), 128)]
    value = note_ref[...].astype(BF)
    for g in range(out_ref.shape[0]):
        out_ref[g] = value


def weight_parts(layout, core, arrived, e, pre, mine_ref, other_ref, spot):
    x = jnp.concatenate([window(arrived[n], i, e) for n, i in layout], axis=0)
    part = mm(x, pre, TN)
    half = part.shape[0] // 2
    first, second = part[:half], part[half:]
    mine_ref[0, spot] = jnp.where(core == 0, first, second).astype(BF)
    other_ref[0, spot] = jnp.where(core == 0, second, first).astype(BF)


def first_kernel(layout, arrays, parts, at_ref, recv_ref, down_ref, *refs):
    keeps, ws = refs[:parts], refs[parts : 2 * parts]
    arrived = refs[2 * parts : 2 * parts + arrays]
    pre_ref, mine_ref, other_ref, grad_ref = refs[2 * parts + arrays :]
    ff = down_ref.shape[1]

    def run(e):
        if e == 0:
            for g in range(recv_ref.shape[0]):
                value = recv_ref[g].astype(F32)
                for c in range(grad_ref.shape[1] // 128):
                    grad_ref[g * SEQS : (g + 1) * SEQS, c * 128 : (c + 1) * 128] = value[c * SEQS : (c + 1) * SEQS]
        back = mm(grad_ref[...].astype(BF), down_ref[0], NT)
        high, low = split2(back)
        two = jnp.concatenate([high, low], axis=0)
        start = 0
        for keep_ref, w_ref in zip(keeps, ws):
            weights = w_ref[0]
            end = start + weights.shape[1]
            inner = mm(jnp.concatenate([weights, weights], axis=0), two, TN)
            pre_ref[0, start:end, 0:ff] = (inner * keep_ref[0, :, 0:ff].astype(F32)).astype(BF)
            pre_ref[0, start:end, ff : 2 * ff] = (inner * keep_ref[0, :, ff : 2 * ff].astype(F32)).astype(BF)
            start = end
        weight_parts(layout, at_ref[2], arrived, e, pre_ref[0], mine_ref, other_ref, 0)

    @pl.when(pl.program_id(0) == 0)
    def _():
        run(0)

    @pl.when(pl.program_id(0) == 1)
    def _():
        run(1)


def more_kernel(layout, arrays, at_ref, pre_ref, *refs):
    for e in range(pre_ref.shape[0]):
        weight_parts(layout, at_ref[2], refs[:arrays], e, pre_ref[e], *refs[arrays:], e)


def body(hidden, w_gate, w_up, w_down, expert_ids, route_weight, seq_len, positive):
    dp, ep = ("z", "core"), ("x", "y")
    tok, width = hidden.shape
    local, _, ff = w_gate.shape
    groups = lax.axis_size(ep)
    members = lax.axis_size(dp)
    top = expert_ids.shape[1]
    length = tok // SEQS
    owned = groups * SEQS
    packed = SEQS * width // 128
    rows = groups * WIN
    me = lax.axis_index(dp).astype(I32).reshape(1)
    smem = pl.BlockSpec(memory_space=pltpu.SMEM)

    def limit(mib):
        return pltpu.CompilerParams(vmem_limit_bytes=mib * 1024 * 1024)

    big = pltpu.CompilerParams(vmem_limit_bytes=50 * 1024 * 1024)

    at = jnp.stack([lax.axis_index(a) for a in ("x", "y", "core", "z")]).astype(I32)
    vmem = pl.BlockSpec(memory_space=pltpu.VMEM)
    message, hidden_sum = pl.pallas_call(
        functools.partial(prepare_kernel, length),
        out_shape=(
            jax.ShapeDtypeStruct((tok + NOTE, width), BF),
            jax.ShapeDtypeStruct((8, width), F32),
        ),
        in_specs=[smem, vmem, vmem, vmem],
        out_specs=(vmem, vmem),
        name="prepare",
    )(seq_len, expert_ids.T, route_weight.T, hidden)

    def ahead(value, k, turned):
        pairs = []
        for core in range(2):
            for x in range(LINE):
                for y in range(LINE):
                    to = ((x + k) % LINE, y) if core == turned else (x, (y + k) % LINE)
                    pairs.append(((core * LINE + x) * LINE + y, (core * LINE + to[0]) * LINE + to[1]))
        return lax.ppermute(value, ("core", "x", "y"), pairs)

    def select(name, halves, *messages):
        count = 1 if halves else 3
        sizes = (1, 1, 1, 1) if halves else (3, 3, 2, 3, 1)
        return pl.pallas_call(
            functools.partial(select_kernel, halves),
            grid=(count,),
            out_shape=[jax.ShapeDtypeStruct((n, PART, width), BF) for n in sizes],
            in_specs=[smem] + [pl.BlockSpec(v.shape, lambda m: (0, 0)) for v in messages],
            out_specs=[
                pl.BlockSpec((1, PART, width), lambda m, n=n: (jnp.minimum(m, n - 1), 0, 0)) for n in sizes
            ],
            cost_estimate=pl.CostEstimate(
                flops=count * LINE * PART * 2 * tok * width,
                bytes_accessed=count * 2 * width * (tok + LINE * PART),
                transcendentals=0,
            ),
            compiler_params=limit(28),
            name=name,
        )(at, *messages)

    cut = (tok + NOTE) // 2
    one, three = ahead(message, 1, 0), ahead(message, 3, 0)
    two = ahead(one[:cut], 1, 0), ahead(three[cut:], 3, 0)
    here, plus, relay, minus, back = select("select_near", False, message, one, three)
    plus, minus = ahead(plus, 1, 1), ahead(minus, 3, 1)
    relay, back = ahead(relay, 1, 1), ahead(back, 3, 1)

    def near_blocks(array, k):
        return [(array, i, m, k) for i, m in enumerate((0, 1, 3))]

    keeps, weights = [], []

    def forward(part, last, arrays, layout, summed):
        rows = len(layout) * WIN
        matrix = pl.BlockSpec((1, width, ff), lambda e: (e, 0, 0))
        sums = pl.BlockSpec((owned, ff), lambda e: (0, e))
        out_shape = [
            jax.ShapeDtypeStruct((owned, local * ff), BF if last else F32),
            pltpu.HBM((local, rows, 2 * ff), BF),
            pltpu.HBM((local, owned, rows), BF),
        ]
        out_specs = [
            sums,
            pl.BlockSpec((1, rows, 2 * ff), lambda e: (e, 0, 0)),
            pl.BlockSpec((1, owned, rows), lambda e: (e, 0, 0)),
        ]
        in_specs = [smem] + [pl.BlockSpec(v.shape, lambda e: (0, 0, 0)) for v in arrays] + [matrix, matrix]
        operands = [at, *arrays, w_gate, w_up]
        if last:
            in_specs.append(pl.BlockSpec((1, ff, width), lambda e: (e, 0, 0)))
            operands.append(w_down)
            out_shape.append(jax.ShapeDtypeStruct((groups, packed, 128), F32))
            out_specs.append(pl.BlockSpec((groups, packed, 128), lambda e: (0, 0, 0)))
        results = pl.pallas_call(
            functools.partial(forward_kernel, layout, last),
            grid=(local,),
            out_shape=out_shape,
            in_specs=in_specs + [sums],
            out_specs=out_specs,
            scratch_shapes=[pltpu.VMEM((owned, width), F32)] if last else [],
            cost_estimate=pl.CostEstimate(
                flops=local * rows * 4 * width * ff,
                bytes_accessed=local * 4 * width * ff + 4 * rows * width,
                transcendentals=local * rows * ff,
            ),
            compiler_params=limit(32),
            name="forward_%d" % part,
        )(*operands, summed)
        keeps.append(results[1])
        weights.append(results[2])
        return results

    layouts = [near_blocks(0, 0), near_blocks(0, 1) + near_blocks(1, 3)]
    groups_of = [(here,), (plus, minus)]
    summed = forward(0, False, groups_of[0], layouts[0], jnp.zeros((owned, local * ff), F32))[0]
    two, summed = lax.optimization_barrier((two, summed))
    far_here, far_plus, far_back, far_minus = select("select_far", True, *two)
    far_plus, far_minus, far_back = ahead(far_plus, 1, 1), ahead(far_minus, 3, 1), ahead(far_back, 3, 1)
    summed = forward(1, False, groups_of[1], layouts[1], summed)[0]
    relay, back, far_back, summed = lax.optimization_barrier((relay, back, far_back, summed))
    relay, back, far_back = ahead(relay, 1, 1), ahead(back, 3, 1), ahead(far_back, 3, 1)
    groups_of.append((relay, back, far_plus, far_back, far_minus, far_here))
    layouts.append(
        [(0, 0, 0, 2), (0, 1, 1, 2), (1, 0, 3, 2), (2, 0, 2, 1), (3, 0, 2, 2), (4, 0, 2, 3), (5, 0, 2, 0)]
    )
    results = forward(2, True, groups_of[2], layouts[2], summed)
    summed = results[0]
    partial = results[3]
    rows = groups * WIN
    arrived, layout = [], []
    for arrays, blocks in zip(groups_of, layouts):
        layout += [(len(arrived) + n, i) for n, i, _, _ in blocks]
        arrived += arrays

    all_summed = lax.all_gather(summed, dp, axis=0, tiled=True)
    returned = lax.all_to_all(partial, ep, split_axis=0, concat_axis=0, tiled=True)

    pooled = pl.pallas_call(
        pool_kernel,
        out_shape=jax.ShapeDtypeStruct((members, packed + NOTE, 128), BF),
        in_specs=[smem, smem, vmem, vmem],
        out_specs=vmem,
        scratch_shapes=[pltpu.VMEM((packed + NOTE, 128), F32)],
        compiler_params=limit(8),
        name="pool",
    )(seq_len, positive, returned, hidden_sum)
    column = lax.all_to_all(pooled, dp, split_axis=0, concat_axis=0, tiled=True)

    noted = packed + members * SEQS
    loss, note = pl.pallas_call(
        contrast_kernel,
        out_shape=(
            jax.ShapeDtypeStruct((1, 128), F32),
            jax.ShapeDtypeStruct((groups, noted, 128), BF),
        ),
        in_specs=[smem, vmem],
        out_specs=(vmem, vmem),
        scratch_shapes=[
            pltpu.VMEM((members * SEQS, width), F32),
            pltpu.VMEM((members, SEQS, width), F32),
            pltpu.VMEM((noted, 128), F32),
        ],
        compiler_params=limit(12),
        name="contrast",
    )(me, column)
    spread = lax.all_to_all(note, ep, split_axis=0, concat_axis=0, tiled=True)
    columns = spread[:, packed:].reshape(groups, members, SEQS, 128)
    columns = jnp.transpose(columns, (1, 0, 2, 3)).reshape(members * owned, 128)

    ring = lax.axis_size("z")
    cols = width // ring
    piece = (local, cols // 2, 2 * ff)

    def shard_spec(order):
        return [
            pl.BlockSpec((v.shape[0], PART, cols), lambda i, at: (0, 0, (at[3] + order(i)) & (ring - 1)))
            for v in arrived
        ]

    def parts_spec():
        return pl.BlockSpec((1,) + piece, lambda i, at: (i, 0, 0, 0))

    def cost(shards, extra=0):
        flops = shards * local * 2 * rows * cols * 2 * ff
        return pl.CostEstimate(flops=flops, bytes_accessed=shards * 4 * local * rows * cols + extra, transcendentals=0)

    pre, mine, other = pl.pallas_call(
        functools.partial(first_kernel, layout, len(arrived), len(keeps)),
        grid_spec=pltpu.PrefetchScalarGridSpec(
            num_scalar_prefetch=1,
            grid=(local,),
            in_specs=[
                pl.BlockSpec((groups, noted, 128), lambda i, at: (0, 0, 0)),
                pl.BlockSpec((1, ff, width), lambda i, at: (i, 0, 0)),
            ]
            + [pl.BlockSpec((1,) + v.shape[1:], lambda i, at: (i, 0, 0)) for v in keeps + weights]
            + shard_spec(lambda i: 4),
            out_specs=[
                pl.BlockSpec((1, rows, 2 * ff), lambda i, at: (i, 0, 0)),
                pl.BlockSpec((1, 1) + piece[1:], lambda i, at: (0, i, 0, 0)),
                pl.BlockSpec((1, 1) + piece[1:], lambda i, at: (0, i, 0, 0)),
            ],
            scratch_shapes=[pltpu.VMEM((owned, width), F32)],
        ),
        out_shape=(
            jax.ShapeDtypeStruct((local, rows, 2 * ff), BF),
            jax.ShapeDtypeStruct((1,) + piece, BF),
            jax.ShapeDtypeStruct((1,) + piece, BF),
        ),
        cost_estimate=cost(1, 16 * 1024 * 1024),
        compiler_params=big,
        name="first_parts",
    )(at, spread, w_down, *keeps, *weights, *arrived)

    def more(shards, order, name):
        return pl.pallas_call(
            functools.partial(more_kernel, layout, len(arrived)),
            grid_spec=pltpu.PrefetchScalarGridSpec(
                num_scalar_prefetch=1,
                grid=(shards,),
                in_specs=[pl.BlockSpec((local, rows, 2 * ff), lambda i, at: (0, 0, 0))] + shard_spec(order),
                out_specs=[parts_spec(), parts_spec()],
            ),
            out_shape=[jax.ShapeDtypeStruct((shards,) + piece, BF)] * 2,
            cost_estimate=cost(shards),
            compiler_params=big,
            name=name,
        )(at, pre, *arrived)

    def swap(value):
        return lax.ppermute(value, "core", [(0, 1), (1, 0)])

    def along(value, k):
        return lax.ppermute(value, "z", [(i, (i + k) % ring) for i in range(ring)])

    def total(*values):
        return sum(v.astype(F32) for v in values)

    theirs = swap(other)
    held, sent = more(2, lambda i: 3 + 2 * i, "parts_three")
    up, down = total(mine[0, 0], theirs[0, 0]).astype(BF), total(mine[0, 1], theirs[0, 1]).astype(BF)
    up, down, pre, sent, all_summed = lax.optimization_barrier((up, down, pre, sent, all_summed))
    up, down, got = along(up, 1), along(down, -1), swap(sent)
    later = more(2, lambda i: 2 + 4 * i, "parts_two")
    up = jnp.stack([total(held[0, 0], got[0, 0], up), total(held[0, 1], got[0, 1])]).astype(BF)
    down = jnp.stack([total(held[1, 0], got[1, 0]), total(held[1, 1], got[1, 1], down)]).astype(BF)
    up, down, pre, later = lax.optimization_barrier((up, down, pre, later))
    held, sent = later
    up, down, got = along(up, 1), along(down, -1), swap(sent)
    later = more(3, lambda i: jnp.where(i == 0, 1, 7 * (2 - i)), "parts_one")
    up = total(held[0], got[0], up).astype(BF)
    down = total(held[1], got[1], down).astype(BF)
    up, down, later = lax.optimization_barrier((up, down, later))
    held, sent = later
    up, down, got = along(up, 1), along(down, -1), swap(sent)
    up = total(held[0], got[0], up).astype(BF)
    down = total(held[1], got[1], down).astype(BF)
    up, down = lax.optimization_barrier((up, down))
    up, down = along(up, 1), along(down, -1)
    grad_gate, grad_up = [
        total(held[2, :, :, s], got[2, :, :, s], up[:, :, s], down[:, :, s])
        for s in (slice(0, ff), slice(ff, 2 * ff))
    ]
    grad_down = jnp.einsum(
        "qef,qd->efd",
        all_summed.reshape(members * owned, local, ff),
        columns,
        preferred_element_type=F32,
    )
    return (
        loss[0, :1],
        grad_gate,
        grad_up,
        grad_down,
    )


def solution(mesh):
    mesh = Mesh(mesh.devices.reshape(8, 2, 4, 4), ("z", "core", "x", "y"))
    dp, ep = ("z", "core"), ("x", "y")
    tokens = P(dp + ep)
    placed = (
        P(dp + ep, None),
        P(ep, None, None),
        P(ep, None, None),
        P(ep, None, None),
        P(dp + ep, None),
        P(dp + ep, None),
        tokens,
        tokens,
    )
    return jax.shard_map(
        body,
        mesh=mesh,
        in_specs=placed,
        out_specs=(tokens, P(ep, dp, None), P(ep, dp, None), P(ep, None, dp)),
        check_vma=False,
    )
```

```python
import functools

import jax
import jax.numpy as jnp
from jax import lax
from jax.experimental import pallas as pl
from jax.experimental.pallas import tpu as pltpu
from jax.sharding import Mesh
from jax.sharding import PartitionSpec as P

inv_temp = 20.0
loss_scale = 128.0
norm_eps = 1e-06

BF = jnp.bfloat16
F32 = jnp.float32
I32 = jnp.int32

PART = 80
WIN = 48
SHIFT = 32
META = 44
SEQS = 3
EXPERTS = 32
LINE = 4
NOTE = 16

NN = (((1,), (0,)), ((), ()))
NT = (((1,), (1,)), ((), ()))
TN = (((0,), (0,)), ((), ()))


def iota(shape, axis):
    return lax.broadcasted_iota(I32, shape, axis)


def mm(a, b, dims=NN):
    return lax.dot_general(a, b, dims, preferred_element_type=F32)


def split2(value):
    high = value.astype(BF)
    return high, (value - high.astype(F32)).astype(BF)


def split3(value):
    high = value.astype(BF)
    rest = value - high.astype(F32)
    mid = rest.astype(BF)
    return high, mid, (rest - mid.astype(F32)).astype(BF)


def third(row):
    return (row * 43) >> 7


def window_row(expert, place):
    odd = (expert & 1) == 1
    return jnp.where(odd, jnp.where(place < 32, place + 16, place - 26), place)


def prepare_kernel(length, len_ref, ids_ref, rw_ref, hid_ref, out_ref, sum_ref):
    top, tok = ids_ref.shape
    experts = EXPERTS
    pos = iota((1, tok), 1)
    seq = jnp.zeros((1, tok), I32)
    bound = jnp.full((1, tok), len_ref[0], I32)
    for s in range(1, len_ref.shape[0]):
        later = pos >= s * length
        seq = seq + later.astype(I32)
        bound = jnp.where(later, len_ref[s], bound)
    valid = pos - seq * length < bound
    ids = jnp.where(valid, ids_ref[...], -1)
    names = iota((experts, tok), 0)
    hits = [(ids[k : k + 1] == names).astype(F32) for k in range(top)]
    count = functools.reduce(jnp.add, hits)
    earlier = (iota((tok, tok), 0) < iota((tok, tok), 1)).astype(BF)
    before = mm(count.astype(BF), earlier)
    weight = rw_ref[...].astype(F32)
    lane = iota((128, tok), 0)
    marks = (seq + 1).astype(F32)
    meta = jnp.zeros((2 * experts, 128), F32)
    spots = []
    for k in range(top):
        place = jnp.sum(hits[k] * before, axis=0, keepdims=True).astype(I32)
        for m in range(k):
            place = place + (ids[m : m + 1] == ids[k : k + 1]).astype(I32)
        spot = window_row(ids[k : k + 1], place)
        spots.append(spot)
        chosen = (lane == spot).astype(BF)
        both = jnp.concatenate([hits[k] * weight[k : k + 1], hits[k] * marks], axis=0)
        meta = meta + mm(both.astype(BF), chosen, NT)
    meta = meta.astype(BF)
    member = jnp.logical_and(iota((8, tok), 0) == seq, valid).astype(BF)
    sum_ref[...] = mm(member, hid_ref[...])
    note = jnp.concatenate([ids.astype(F32), jnp.concatenate(spots, axis=0).astype(F32)], axis=0).astype(BF)
    out_ref[:tok, :] = hid_ref[...]
    out_ref[tok:, :] = jnp.zeros((NOTE, hid_ref.shape[1]), BF)
    out_ref[tok:, 0:tok] = note
    for c in range(2 * experts // NOTE):
        out_ref[tok:, 256 + c * 128 : 384 + c * 128] = meta[c * NOTE : (c + 1) * NOTE]


def select_kernel(halves, at_ref, *refs):
    count = 1 if halves else 3
    inputs, outputs = refs[: 2 if halves else count], refs[2 if halves else count :]
    x, y, core = at_ref[0], at_ref[1], at_ref[2]
    m = pl.program_id(0)
    for source in range(count):

        @pl.when(m == source)
        def _(source=source):
            message = inputs[1] if halves else inputs[source]
            at = message.shape[0] - NOTE
            values = message[:at, :]
            if halves:
                values = jnp.concatenate([inputs[0][...], values], axis=0)
            tok = values.shape[0]
            note = message[at:, 0:tok].astype(F32)
            ids = note[0 : NOTE // 2].astype(I32)
            spots = note[NOTE // 2 :].astype(I32)
            device = ids >> 1
            row = (ids & 1) * SHIFT + spots
            line = iota((PART, tok), 0)
            meta = jnp.concatenate(
                [message[at:, 256 + c * 128 : 384 + c * 128] for c in range(2 * EXPERTS // NOTE)], axis=0
            )
            rows = iota((PART, 2 * EXPERTS), 0)
            col = iota((PART, 2 * EXPERTS), 1)
            mark = (col >= EXPERTS).astype(I32)
            expert = col - EXPERTS * mark
            noted = rows == META + 2 * (expert & 1) + mark
            wanted = []
            chosen = []
            for k in range(LINE):
                j = jnp.where(
                    core == 0,
                    x * LINE + ((y + k) & (LINE - 1)),
                    ((x + k) & (LINE - 1)) * LINE + y,
                )
                spot = jnp.where(device == j, row, -1)
                picked = line == spot[0:1]
                for t in range(1, NOTE // 2):
                    picked = jnp.logical_or(picked, line == spot[t : t + 1])
                wanted.append(picked.astype(BF))
                chosen.append(jnp.logical_and(noted, expert >> 1 == j).astype(BF))
            out = mm(jnp.concatenate(wanted, axis=0), values)
            extra = mm(jnp.concatenate(chosen, axis=0), meta)
            for k in range(LINE):
                part = slice(k * PART, (k + 1) * PART)
                ref = outputs[4 if k == 2 and source == 2 else k]
                ref[0, :, 128:] = out[part, 128:].astype(BF)
                ref[0, :, :128] = (out[part, :128] + extra[part]).astype(BF)


def window(ref, m, h, cols=slice(None)):
    return ref[m, h * SHIFT : h * SHIFT + WIN, cols]


def forward_kernel(layout, last, at_ref, *refs):
    arrays = max(spot[0] for spot in layout) + 1
    arrived = refs[:arrays]
    if last:
        gate_ref, up_ref, down_ref, before_ref, a_ref, keep_ref, w_ref, part_ref, acc_ref = refs[arrays:]
    else:
        gate_ref, up_ref, before_ref, a_ref, keep_ref, w_ref = refs[arrays:]
    e = pl.program_id(0)
    here_x, here_y, core = at_ref[0], at_ref[1], at_ref[2]
    blocks = len(layout)
    rows = blocks * WIN
    owned = before_ref.shape[0]
    groups = owned // SEQS

    def run(h):
        x = jnp.concatenate([window(arrived[n], i, h) for n, i, _, _ in layout], axis=0)
        gate = mm(x, gate_ref[0])
        up = mm(x, up_ref[0])
        sigma = jax.nn.sigmoid(gate)
        act = gate * sigma
        slope = sigma * (1.0 + gate * (1.0 - sigma))
        ff = gate.shape[1]
        keep_ref[0, :, 0:ff] = (up * slope).astype(BF)
        keep_ref[0, :, ff : 2 * ff] = act.astype(BF)
        inner = (act * up).astype(BF)
        at = META - 32 + 2 * h
        tails = [arrived[n][i, 32:48, 0:128].astype(F32) for n, i, _, _ in layout]
        pad = [jnp.zeros((8 - blocks, 128), F32)]
        wrow = jnp.concatenate([t[at : at + 1] for t in tails] + pad, axis=0).astype(BF)
        srow = jnp.concatenate([t[at + 1 : at + 2] for t in tails] + pad, axis=0).astype(BF)
        col8 = iota((owned, 8), 1)
        col = iota((owned, rows), 1)
        home8 = jnp.full((owned, 8), -1, I32)
        home = jnp.full((owned, rows), -1, I32)
        for r, (_, _, m, k) in enumerate(layout):
            first, second = (here_x - m) & 3, (here_y - k) & 3
            third_, fourth = (here_x - k) & 3, (here_y - m) & 3
            j = jnp.where(core == 0, first * LINE + second, third_ * LINE + fourth)
            home8 = jnp.where(col8 == r, j, home8)
            home = jnp.where(col >= r * WIN, j, home)
        owner = (third(iota((owned, 8), 0)) == home8).astype(BF)
        wrep = mm(owner, wrow)
        srep = mm(owner, srow)
        row = iota((owned, 128), 0)
        number = (row - SEQS * third(row) + 1).astype(F32)
        picked = jnp.where(srep == number, wrep, 0.0).astype(BF)
        place = iota((128, rows), 1)
        place = place - WIN * ((place * 683) >> 15)
        spread = (place == iota((128, rows), 0)).astype(BF)
        inside = third(iota((owned, rows), 0)) == home
        weights = jnp.where(inside, mm(picked, spread), 0.0).astype(BF)
        w_ref[0] = weights
        a = before_ref[...] + mm(weights, inner)
        if not last:
            a_ref[...] = a
            return
        high, low = split2(a)
        a_ref[...] = high
        both = mm(jnp.concatenate([high, low], axis=0), down_ref[0])
        total = both[:owned] + both[owned:]
        if h == 0:
            acc_ref[...] = total
        else:
            total = total + acc_ref[...]
            for g in range(groups):
                for c in range(total.shape[1] // 128):
                    part_ref[g, c * SEQS : (c + 1) * SEQS, :] = total[
                        g * SEQS : (g + 1) * SEQS, c * 128 : (c + 1) * 128
                    ]

    @pl.when(e == 0)
    def _():
        run(0)

    @pl.when(e == 1)
    def _():
        run(1)


def pool_kernel(len_ref, pos_ref, recv_ref, sum_ref, out_ref, note_ref):
    groups, packed, _ = recv_ref.shape
    chunks = packed // SEQS
    total = recv_ref[0]
    for g in range(1, groups):
        total = total + recv_ref[g]
    note_ref[0:packed, :] = total
    total = jnp.concatenate([note_ref[c * SEQS : (c + 1) * SEQS, :] for c in range(chunks)], axis=1)
    row = iota((SEQS, 1), 0)
    inverse = jnp.zeros((SEQS, 1), F32)
    for s in range(SEQS):
        inverse = jnp.where(row == s, 1.0 / jnp.full((SEQS, 1), len_ref[s], I32).astype(F32), inverse)
    pooled = (total + sum_ref[0:SEQS, :]) * inverse
    scale = lax.rsqrt(jnp.sum(pooled * pooled, axis=1, keepdims=True) + norm_eps)
    positive = pos_ref[0]
    col = iota((1, 128), 1)
    note = jnp.where(col == 0, (positive >> 1) * SEQS + 1 + (positive & 1), 0)
    for s in range(SEQS):
        note = jnp.where(col == 1 + s, len_ref[s], note)
    note = note.astype(F32)
    for place, piece in enumerate(split3(scale)):
        piece = piece.astype(F32)
        for s in range(SEQS):
            note = jnp.where(col == 4 * (place + 1) + 1 + s, piece[s : s + 1], note)
    embed = pooled * scale
    for c in range(chunks):
        note_ref[c * SEQS : (c + 1) * SEQS, :] = embed[:, c * 128 : (c + 1) * 128]
    note_ref[packed:, :] = jnp.where(iota((NOTE, 128), 0) == 0, note, 0.0)
    value = note_ref[...].astype(BF)
    for g in range(groups):
        out_ref[g] = value


def contrast_kernel(at_ref, recv_ref, loss_ref, out_ref, all_ref, grad_ref, note_ref):
    groups = recv_ref.shape[0]
    packed = recv_ref.shape[1] - NOTE
    chunks = packed // SEQS
    owned = groups * SEQS
    me = at_ref[0]
    notes = []
    for g in range(groups):
        value = recv_ref[g].astype(F32)
        notes.append(value[packed : packed + 1])
        for c in range(chunks):
            all_ref[g * SEQS : (g + 1) * SEQS, c * 128 : (c + 1) * 128] = value[c * SEQS : (c + 1) * SEQS]
    notes = jnp.concatenate(notes, axis=0).astype(BF)

    def sort(shape, axis):
        place = iota(shape, axis)
        return place - SEQS * third(place)

    owner = (third(iota((owned, groups), 0)) == iota((owned, groups), 1)).astype(BF)
    notes = mm(owner, notes)
    lane = iota((owned, 128), 1)
    sub = sort((owned, 128), 0)
    target = jnp.sum(jnp.where(lane == 0, notes, 0.0), axis=1, keepdims=True)
    length = jnp.sum(jnp.where(lane == 1 + sub, notes, 0.0), axis=1, keepdims=True)
    pieces = jnp.logical_and(lane > 4, lane < 16)
    scale = jnp.sum(jnp.where(jnp.logical_and(pieces, (lane & 3) == 1 + sub), notes, 0.0), axis=1, keepdims=True)
    wide = all_ref[...]
    embed = wide.astype(BF)
    scores = mm(embed, embed, NT) * inv_temp
    passage = sort((owned, owned), 1) > 0
    total = jnp.log(jnp.sum(jnp.where(passage, jnp.exp(scores), 0.0), axis=1, keepdims=True))
    hit = (iota((owned, owned), 1).astype(F32) == target).astype(F32)
    losses = total - jnp.sum(hit * scores, axis=1, keepdims=True)
    wanted = iota((owned, 128), 0) == me * SEQS
    loss_ref[...] = jnp.sum(jnp.where(wanted, losses, 0.0), axis=0, keepdims=True)
    coeff = (jnp.where(passage, jnp.exp(scores - total), 0.0) - hit) * (loss_scale * inv_temp)
    coeff = jnp.where(sort((owned, owned), 0) == 0, coeff, 0.0)
    coeff = coeff + coeff.T
    three = mm(jnp.concatenate(split3(coeff), axis=0), embed)
    grad = three[:owned] + three[owned : 2 * owned] + three[2 * owned :]
    along = jnp.sum(wide * grad, axis=1, keepdims=True)
    grad = (grad - wide * along) * (scale / length)
    for g in range(groups):
        grad_ref[g] = grad[g * SEQS : (g + 1) * SEQS]
    own = grad_ref[me]
    for c in range(chunks):
        note_ref[c * SEQS : (c + 1) * SEQS, :] = own[:, c * 128 : (c + 1) * 128]
    for r in range(groups // 2):
        z = (((me >> 1) + (0, -2, 2, 4)[r // 2]) & (groups // 2 - 1)) ^ (r % 2)
        i = 2 * z + (me & 1)
        for h in range(2):
            here = pl.ds(pl.multiple_of((me ^ h) * 128, 128), 128)
            spot = packed + (2 * r + h) * SEQS
            note_ref[spot : spot + SEQS, :] = grad_ref[i, :, here]
    value = note_ref[...].astype(BF)
    for g in range(out_ref.shape[0]):
        out_ref[g] = value


def weight_parts(layout, core, arrived, e, pre, mine_ref, other_ref, spot):
    x = jnp.concatenate([window(arrived[n], i, e) for n, i in layout], axis=0)
    part = mm(x, pre, TN)
    half = part.shape[0] // 2
    first, second = part[:half], part[half:]
    mine_ref[0, spot] = jnp.where(core == 0, first, second).astype(BF)
    other_ref[0, spot] = jnp.where(core == 0, second, first).astype(BF)


def first_kernel(layout, arrays, parts, at_ref, recv_ref, down_ref, *refs):
    keeps, ws = refs[:parts], refs[parts : 2 * parts]
    arrived = refs[2 * parts : 2 * parts + arrays]
    pre_ref, mine_ref, other_ref, grad_ref = refs[2 * parts + arrays :]
    ff = down_ref.shape[1]

    def run(e):
        if e == 0:
            for g in range(recv_ref.shape[0]):
                value = recv_ref[g].astype(F32)
                for c in range(grad_ref.shape[1] // 128):
                    grad_ref[g * SEQS : (g + 1) * SEQS, c * 128 : (c + 1) * 128] = value[c * SEQS : (c + 1) * SEQS]
        back = mm(grad_ref[...].astype(BF), down_ref[0], NT)
        high, low = split2(back)
        two = jnp.concatenate([high, low], axis=0)
        start = 0
        for keep_ref, w_ref in zip(keeps, ws):
            weights = w_ref[0]
            end = start + weights.shape[1]
            inner = mm(jnp.concatenate([weights, weights], axis=0), two, TN)
            pre_ref[0, start:end, 0:ff] = (inner * keep_ref[0, :, 0:ff].astype(F32)).astype(BF)
            pre_ref[0, start:end, ff : 2 * ff] = (inner * keep_ref[0, :, ff : 2 * ff].astype(F32)).astype(BF)
            start = end
        weight_parts(layout, at_ref[2], arrived, e, pre_ref[0], mine_ref, other_ref, 0)

    @pl.when(pl.program_id(0) == 0)
    def _():
        run(0)

    @pl.when(pl.program_id(0) == 1)
    def _():
        run(1)


def more_kernel(layout, arrays, at_ref, pre_ref, *refs):
    for e in range(pre_ref.shape[0]):
        weight_parts(layout, at_ref[2], refs[:arrays], e, pre_ref[e], *refs[arrays:], e)


def down_kernel(recv_ref, *refs):
    pairs, (mine_ref, other_ref, grad_ref) = refs[:4], refs[4:]
    groups = recv_ref.shape[0]
    owned = pairs[0].shape[1]
    both = 2 * owned
    packed = recv_ref.shape[1] - 16 * SEQS
    for g in range(groups):
        value = recv_ref[g].astype(F32)
        for r in range(8):
            for h in range(2):
                spot = packed + (2 * r + h) * SEQS
                row = r * owned + g * SEQS
                grad_ref[row : row + SEQS, h * 128 : (h + 1) * 128] = value[spot : spot + SEQS]
    grad = grad_ref[...].astype(BF)
    total = sum(
        mm(ref[...].reshape(both, -1), grad[n * both : (n + 1) * both], TN) for n, ref in enumerate(pairs)
    )
    mine_ref[...] = total[:, :128]
    other_ref[...] = total[:, 128:]


def body(hidden, w_gate, w_up, w_down, expert_ids, route_weight, seq_len, positive):
    dp, ep = ("z", "core"), ("x", "y")
    tok, width = hidden.shape
    local, _, ff = w_gate.shape
    groups = lax.axis_size(ep)
    members = lax.axis_size(dp)
    top = expert_ids.shape[1]
    length = tok // SEQS
    owned = groups * SEQS
    packed = SEQS * width // 128
    rows = groups * WIN
    me = lax.axis_index(dp).astype(I32).reshape(1)
    smem = pl.BlockSpec(memory_space=pltpu.SMEM)

    def limit(mib):
        return pltpu.CompilerParams(vmem_limit_bytes=mib * 1024 * 1024)

    big = pltpu.CompilerParams(vmem_limit_bytes=50 * 1024 * 1024)

    at = jnp.stack([lax.axis_index(a) for a in ("x", "y", "core", "z")]).astype(I32)
    vmem = pl.BlockSpec(memory_space=pltpu.VMEM)
    message, hidden_sum = pl.pallas_call(
        functools.partial(prepare_kernel, length),
        out_shape=(
            jax.ShapeDtypeStruct((tok + NOTE, width), BF),
            jax.ShapeDtypeStruct((8, width), F32),
        ),
        in_specs=[smem, vmem, vmem, vmem],
        out_specs=(vmem, vmem),
        name="prepare",
    )(seq_len, expert_ids.T, route_weight.T, hidden)

    def ahead(value, k, turned):
        pairs = []
        for core in range(2):
            for x in range(LINE):
                for y in range(LINE):
                    to = ((x + k) % LINE, y) if core == turned else (x, (y + k) % LINE)
                    pairs.append(((core * LINE + x) * LINE + y, (core * LINE + to[0]) * LINE + to[1]))
        return lax.ppermute(value, ("core", "x", "y"), pairs)

    def select(name, halves, *messages):
        count = 1 if halves else 3
        sizes = (1, 1, 1, 1) if halves else (3, 3, 2, 3, 1)
        return pl.pallas_call(
            functools.partial(select_kernel, halves),
            grid=(count,),
            out_shape=[jax.ShapeDtypeStruct((n, PART, width), BF) for n in sizes],
            in_specs=[smem] + [pl.BlockSpec(v.shape, lambda m: (0, 0)) for v in messages],
            out_specs=[
                pl.BlockSpec((1, PART, width), lambda m, n=n: (jnp.minimum(m, n - 1), 0, 0)) for n in sizes
            ],
            cost_estimate=pl.CostEstimate(
                flops=count * LINE * PART * 2 * tok * width,
                bytes_accessed=count * 2 * width * (tok + LINE * PART),
                transcendentals=0,
            ),
            compiler_params=limit(28),
            name=name,
        )(at, *messages)

    cut = (tok + NOTE) // 2
    one, three = ahead(message, 1, 0), ahead(message, 3, 0)
    two = ahead(one[:cut], 1, 0), ahead(three[cut:], 3, 0)
    here, plus, relay, minus, back = select("select_near", False, message, one, three)
    plus, minus = ahead(plus, 1, 1), ahead(minus, 3, 1)
    relay, back = ahead(relay, 1, 1), ahead(back, 3, 1)

    def near_blocks(array, k):
        return [(array, i, m, k) for i, m in enumerate((0, 1, 3))]

    keeps, weights = [], []

    def forward(part, last, arrays, layout, summed):
        rows = len(layout) * WIN
        matrix = pl.BlockSpec((1, width, ff), lambda e: (e, 0, 0))
        sums = pl.BlockSpec((owned, ff), lambda e: (0, e))
        out_shape = [
            jax.ShapeDtypeStruct((owned, local * ff), BF if last else F32),
            pltpu.HBM((local, rows, 2 * ff), BF),
            pltpu.HBM((local, owned, rows), BF),
        ]
        out_specs = [
            sums,
            pl.BlockSpec((1, rows, 2 * ff), lambda e: (e, 0, 0)),
            pl.BlockSpec((1, owned, rows), lambda e: (e, 0, 0)),
        ]
        in_specs = [smem] + [pl.BlockSpec(v.shape, lambda e: (0, 0, 0)) for v in arrays] + [matrix, matrix]
        operands = [at, *arrays, w_gate, w_up]
        if last:
            in_specs.append(pl.BlockSpec((1, ff, width), lambda e: (e, 0, 0)))
            operands.append(w_down)
            out_shape.append(jax.ShapeDtypeStruct((groups, packed, 128), F32))
            out_specs.append(pl.BlockSpec((groups, packed, 128), lambda e: (0, 0, 0)))
        results = pl.pallas_call(
            functools.partial(forward_kernel, layout, last),
            grid=(local,),
            out_shape=out_shape,
            in_specs=in_specs + [sums],
            out_specs=out_specs,
            scratch_shapes=[pltpu.VMEM((owned, width), F32)] if last else [],
            cost_estimate=pl.CostEstimate(
                flops=local * rows * 4 * width * ff,
                bytes_accessed=local * 4 * width * ff + 4 * rows * width,
                transcendentals=local * rows * ff,
            ),
            compiler_params=limit(32),
            name="forward_%d" % part,
        )(*operands, summed)
        keeps.append(results[1])
        weights.append(results[2])
        return results

    layouts = [near_blocks(0, 0), near_blocks(0, 1) + near_blocks(1, 3)]
    groups_of = [(here,), (plus, minus)]
    summed = forward(0, False, groups_of[0], layouts[0], jnp.zeros((owned, local * ff), F32))[0]
    two, summed = lax.optimization_barrier((two, summed))
    far_here, far_plus, far_back, far_minus = select("select_far", True, *two)
    far_plus, far_minus, far_back = ahead(far_plus, 1, 1), ahead(far_minus, 3, 1), ahead(far_back, 3, 1)
    summed = forward(1, False, groups_of[1], layouts[1], summed)[0]
    relay, back, far_back, summed = lax.optimization_barrier((relay, back, far_back, summed))
    relay, back, far_back = ahead(relay, 1, 1), ahead(back, 3, 1), ahead(far_back, 3, 1)
    groups_of.append((relay, back, far_plus, far_back, far_minus, far_here))
    layouts.append(
        [(0, 0, 0, 2), (0, 1, 1, 2), (1, 0, 3, 2), (2, 0, 2, 1), (3, 0, 2, 2), (4, 0, 2, 3), (5, 0, 2, 0)]
    )
    results = forward(2, True, groups_of[2], layouts[2], summed)
    summed = results[0]
    partial = results[3]
    rows = groups * WIN
    arrived, layout = [], []
    for arrays, blocks in zip(groups_of, layouts):
        layout += [(len(arrived) + n, i) for n, i, _, _ in blocks]
        arrived += arrays

    returned = lax.all_to_all(partial, ep, split_axis=0, concat_axis=0, tiled=True)

    ring = lax.axis_size("z")

    def across(value, k):
        return lax.ppermute(value, "z", [(i, i ^ k) for i in range(ring)])

    def along(value, k):
        return lax.ppermute(value, "z", [(i, (i + k) % ring) for i in range(ring)])

    one_sum = across(summed, 1)
    returned, one_sum = lax.optimization_barrier((returned, one_sum))
    pair = jnp.stack([summed, one_sum])

    pooled = pl.pallas_call(
        pool_kernel,
        out_shape=jax.ShapeDtypeStruct((members, packed + NOTE, 128), BF),
        in_specs=[smem, smem, vmem, vmem],
        out_specs=vmem,
        scratch_shapes=[pltpu.VMEM((packed + NOTE, 128), F32)],
        compiler_params=limit(8),
        name="pool",
    )(seq_len, positive, returned, hidden_sum)
    column = lax.all_to_all(pooled, dp, split_axis=0, concat_axis=0, tiled=True)
    below, above = along(pair, 2), along(pair, -2)
    column, below, above = lax.optimization_barrier((column, below, above))
    far_sums = along(below, 2)

    noted = packed + members * SEQS
    loss, note = pl.pallas_call(
        contrast_kernel,
        out_shape=(
            jax.ShapeDtypeStruct((1, 128), F32),
            jax.ShapeDtypeStruct((groups, noted, 128), BF),
        ),
        in_specs=[smem, vmem],
        out_specs=(vmem, vmem),
        scratch_shapes=[
            pltpu.VMEM((members * SEQS, width), F32),
            pltpu.VMEM((members, SEQS, width), F32),
            pltpu.VMEM((noted, 128), F32),
        ],
        compiler_params=limit(12),
        name="contrast",
    )(me, column)
    spread = lax.all_to_all(note, ep, split_axis=0, concat_axis=0, tiled=True)
    spread, far_sums = lax.optimization_barrier((spread, far_sums))
    cols = width // ring
    piece = (local, cols // 2, 2 * ff)

    def shard_spec(order):
        return [
            pl.BlockSpec((v.shape[0], PART, cols), lambda i, at: (0, 0, (at[3] + order(i)) & (ring - 1)))
            for v in arrived
        ]

    def parts_spec():
        return pl.BlockSpec((1,) + piece, lambda i, at: (i, 0, 0, 0))

    def cost(shards, extra=0):
        flops = shards * local * 2 * rows * cols * 2 * ff
        return pl.CostEstimate(flops=flops, bytes_accessed=shards * 4 * local * rows * cols + extra, transcendentals=0)

    pre, mine, other = pl.pallas_call(
        functools.partial(first_kernel, layout, len(arrived), len(keeps)),
        grid_spec=pltpu.PrefetchScalarGridSpec(
            num_scalar_prefetch=1,
            grid=(local,),
            in_specs=[
                pl.BlockSpec((groups, noted, 128), lambda i, at: (0, 0, 0)),
                pl.BlockSpec((1, ff, width), lambda i, at: (i, 0, 0)),
            ]
            + [pl.BlockSpec((1,) + v.shape[1:], lambda i, at: (i, 0, 0)) for v in keeps + weights]
            + shard_spec(lambda i: 4),
            out_specs=[
                pl.BlockSpec((1, rows, 2 * ff), lambda i, at: (i, 0, 0)),
                pl.BlockSpec((1, 1) + piece[1:], lambda i, at: (0, i, 0, 0)),
                pl.BlockSpec((1, 1) + piece[1:], lambda i, at: (0, i, 0, 0)),
            ],
            scratch_shapes=[pltpu.VMEM((owned, width), F32)],
        ),
        out_shape=(
            jax.ShapeDtypeStruct((local, rows, 2 * ff), BF),
            jax.ShapeDtypeStruct((1,) + piece, BF),
            jax.ShapeDtypeStruct((1,) + piece, BF),
        ),
        cost_estimate=cost(1, 16 * 1024 * 1024),
        compiler_params=big,
        name="first_parts",
    )(at, spread, w_down, *keeps, *weights, *arrived)

    def more(shards, order, name):
        return pl.pallas_call(
            functools.partial(more_kernel, layout, len(arrived)),
            grid_spec=pltpu.PrefetchScalarGridSpec(
                num_scalar_prefetch=1,
                grid=(shards,),
                in_specs=[pl.BlockSpec((local, rows, 2 * ff), lambda i, at: (0, 0, 0))] + shard_spec(order),
                out_specs=[parts_spec(), parts_spec()],
            ),
            out_shape=[jax.ShapeDtypeStruct((shards,) + piece, BF)] * 2,
            cost_estimate=cost(shards),
            compiler_params=big,
            name=name,
        )(at, pre, *arrived)

    def swap(value):
        return lax.ppermute(value, "core", [(0, 1), (1, 0)])

    def total(*values):
        return sum(v.astype(F32) for v in values)

    theirs = swap(other)
    held, sent = more(2, lambda i: 3 + 2 * i, "parts_three")
    up, down = total(mine[0, 0], theirs[0, 0]).astype(BF), total(mine[0, 1], theirs[0, 1]).astype(BF)
    up, down, pre, sent = lax.optimization_barrier((up, down, pre, sent))
    up, down, got = along(up, 1), along(down, -1), swap(sent)
    later = more(2, lambda i: 2 + 4 * i, "parts_two")
    up = jnp.stack([total(held[0, 0], got[0, 0], up), total(held[0, 1], got[0, 1])]).astype(BF)
    down = jnp.stack([total(held[1, 0], got[1, 0]), total(held[1, 1], got[1, 1], down)]).astype(BF)
    up, down, pre, later = lax.optimization_barrier((up, down, pre, later))
    held, sent = later
    up, down, got = along(up, 1), along(down, -1), swap(sent)
    later = more(3, lambda i: jnp.where(i == 0, 1, 7 * (2 - i)), "parts_one")
    up = total(held[0], got[0], up).astype(BF)
    down = total(held[1], got[1], down).astype(BF)
    up, down, later, far_sums = lax.optimization_barrier((up, down, later, far_sums))
    held, sent = later
    up, down, got = along(up, 1), along(down, -1), swap(sent)
    up = total(held[0], got[0], up).astype(BF)
    down = total(held[1], got[1], down).astype(BF)
    up, down = lax.optimization_barrier((up, down))
    up, down = along(up, 1), along(down, -1)
    grad_gate, grad_up = [
        total(held[2, :, :, s], got[2, :, :, s], up[:, :, s], down[:, :, s])
        for s in (slice(0, ff), slice(ff, 2 * ff))
    ]
    down_mine, down_other = pl.pallas_call(
        down_kernel,
        out_shape=[jax.ShapeDtypeStruct((local * ff, 128), F32)] * 2,
        in_specs=[vmem] * 5,
        out_specs=[vmem, vmem],
        scratch_shapes=[pltpu.VMEM((ring * owned, 256), F32)],
        cost_estimate=pl.CostEstimate(
            flops=2 * ring * owned * local * ff * 256, bytes_accessed=4 * 1024 * 1024, transcendentals=0
        ),
        compiler_params=limit(12),
        name="down",
    )(spread, pair, below, above, far_sums)
    grad_down = (down_mine + swap(down_other)).reshape(local, ff, 128)
    return (
        loss[0, :1],
        grad_gate,
        grad_up,
        grad_down,
    )


def solution(mesh):
    mesh = Mesh(mesh.devices.reshape(8, 2, 4, 4), ("z", "core", "x", "y"))
    dp, ep = ("z", "core"), ("x", "y")
    tokens = P(dp + ep)
    placed = (
        P(dp + ep, None),
        P(ep, None, None),
        P(ep, None, None),
        P(ep, None, None),
        P(dp + ep, None),
        P(dp + ep, None),
        tokens,
        tokens,
    )
    return jax.shard_map(
        body,
        mesh=mesh,
        in_specs=placed,
        out_specs=(tokens, P(ep, dp, None), P(ep, dp, None), P(ep, None, dp)),
        check_vma=False,
    )
```

```python
import functools

import jax
import jax.numpy as jnp
from jax import lax
from jax.experimental import pallas as pl
from jax.experimental.pallas import tpu as pltpu
from jax.sharding import Mesh
from jax.sharding import PartitionSpec as P

inv_temp = 20.0
loss_scale = 128.0
norm_eps = 1e-06

BF = jnp.bfloat16
F32 = jnp.float32
I32 = jnp.int32

PART = 80
WIN = 48
SHIFT = 32
META = 44
SEQS = 3
EXPERTS = 32
LINE = 4
NOTE = 16

NN = (((1,), (0,)), ((), ()))
NT = (((1,), (1,)), ((), ()))
TN = (((0,), (0,)), ((), ()))


def iota(shape, axis):
    return lax.broadcasted_iota(I32, shape, axis)


def mm(a, b, dims=NN):
    return lax.dot_general(a, b, dims, preferred_element_type=F32)


def split2(value):
    high = value.astype(BF)
    return high, (value - high.astype(F32)).astype(BF)


def split3(value):
    high = value.astype(BF)
    rest = value - high.astype(F32)
    mid = rest.astype(BF)
    return high, mid, (rest - mid.astype(F32)).astype(BF)


def third(row):
    return (row * 43) >> 7


def window_row(expert, place):
    odd = (expert & 1) == 1
    return jnp.where(odd, jnp.where(place < 32, place + 16, place - 26), place)


def prepare_kernel(length, len_ref, ids_ref, rw_ref, hid_ref, out_ref, sum_ref):
    top, tok = ids_ref.shape
    experts = EXPERTS
    pos = iota((1, tok), 1)
    seq = jnp.zeros((1, tok), I32)
    bound = jnp.full((1, tok), len_ref[0], I32)
    for s in range(1, len_ref.shape[0]):
        later = pos >= s * length
        seq = seq + later.astype(I32)
        bound = jnp.where(later, len_ref[s], bound)
    valid = pos - seq * length < bound
    ids = jnp.where(valid, ids_ref[...], -1)
    names = iota((experts, tok), 0)
    hits = [(ids[k : k + 1] == names).astype(F32) for k in range(top)]
    count = functools.reduce(jnp.add, hits)
    earlier = (iota((tok, tok), 0) < iota((tok, tok), 1)).astype(BF)
    before = mm(count.astype(BF), earlier)
    weight = rw_ref[...].astype(F32)
    lane = iota((128, tok), 0)
    marks = (seq + 1).astype(F32)
    meta = jnp.zeros((2 * experts, 128), F32)
    spots = []
    for k in range(top):
        place = jnp.sum(hits[k] * before, axis=0, keepdims=True).astype(I32)
        for m in range(k):
            place = place + (ids[m : m + 1] == ids[k : k + 1]).astype(I32)
        spot = window_row(ids[k : k + 1], place)
        spots.append(spot)
        chosen = (lane == spot).astype(BF)
        both = jnp.concatenate([hits[k] * weight[k : k + 1], hits[k] * marks], axis=0)
        meta = meta + mm(both.astype(BF), chosen, NT)
    meta = meta.astype(BF)
    member = jnp.logical_and(iota((8, tok), 0) == seq, valid).astype(BF)
    sum_ref[...] = mm(member, hid_ref[...])
    note = jnp.concatenate([ids.astype(F32), jnp.concatenate(spots, axis=0).astype(F32)], axis=0).astype(BF)
    out_ref[:tok, :] = hid_ref[...]
    out_ref[tok:, :] = jnp.zeros((NOTE, hid_ref.shape[1]), BF)
    out_ref[tok:, 0:tok] = note
    for c in range(2 * experts // NOTE):
        out_ref[tok:, 256 + c * 128 : 384 + c * 128] = meta[c * NOTE : (c + 1) * NOTE]


def select_kernel(halves, at_ref, *refs):
    count = 1 if halves else 3
    inputs, outputs = refs[: 2 if halves else count], refs[2 if halves else count :]
    x, y, core = at_ref[0], at_ref[1], at_ref[2]
    m = pl.program_id(0)
    for source in range(count):

        @pl.when(m == source)
        def _(source=source):
            message = inputs[1] if halves else inputs[source]
            at = message.shape[0] - NOTE
            values = message[:at, :]
            if halves:
                values = jnp.concatenate([inputs[0][...], values], axis=0)
            tok = values.shape[0]
            note = message[at:, 0:tok].astype(F32)
            ids = note[0 : NOTE // 2].astype(I32)
            spots = note[NOTE // 2 :].astype(I32)
            device = ids >> 1
            row = (ids & 1) * SHIFT + spots
            line = iota((PART, tok), 0)
            meta = jnp.concatenate(
                [message[at:, 256 + c * 128 : 384 + c * 128] for c in range(2 * EXPERTS // NOTE)], axis=0
            )
            rows = iota((PART, 2 * EXPERTS), 0)
            col = iota((PART, 2 * EXPERTS), 1)
            mark = (col >= EXPERTS).astype(I32)
            expert = col - EXPERTS * mark
            noted = rows == META + 2 * (expert & 1) + mark
            wanted = []
            chosen = []
            for k in range(LINE):
                j = jnp.where(
                    core == 0,
                    x * LINE + ((y + k) & (LINE - 1)),
                    ((x + k) & (LINE - 1)) * LINE + y,
                )
                spot = jnp.where(device == j, row, -1)
                picked = line == spot[0:1]
                for t in range(1, NOTE // 2):
                    picked = jnp.logical_or(picked, line == spot[t : t + 1])
                wanted.append(picked.astype(BF))
                chosen.append(jnp.logical_and(noted, expert >> 1 == j).astype(BF))
            out = mm(jnp.concatenate(wanted, axis=0), values)
            extra = mm(jnp.concatenate(chosen, axis=0), meta)
            for k in range(LINE):
                part = slice(k * PART, (k + 1) * PART)
                ref = outputs[4 if k == 2 and source == 2 else k]
                ref[0, :, 128:] = out[part, 128:].astype(BF)
                ref[0, :, :128] = (out[part, :128] + extra[part]).astype(BF)


def window(ref, m, h):
    start = h * SHIFT if isinstance(h, int) else pl.multiple_of(h * SHIFT, 16)
    return ref[m, pl.ds(start, WIN), :]


def forward_kernel(layout, last, at_ref, *refs):
    arrays = max(spot[0] for spot in layout) + 1
    arrived = refs[:arrays]
    if last:
        gate_ref, up_ref, down_ref, before_ref, a_ref, keep_ref, w_ref, part_ref, acc_ref = refs[arrays:]
    else:
        gate_ref, up_ref, before_ref, a_ref, keep_ref, w_ref = refs[arrays:]
    e = pl.program_id(0)
    here_x, here_y, core = at_ref[0], at_ref[1], at_ref[2]
    blocks = len(layout)
    rows = blocks * WIN
    owned = before_ref.shape[0]
    groups = owned // SEQS

    def run(h):
        x = jnp.concatenate([window(arrived[n], i, h) for n, i, _, _ in layout], axis=0)
        gate = mm(x, gate_ref[0])
        up = mm(x, up_ref[0])
        sigma = jax.nn.sigmoid(gate)
        act = gate * sigma
        slope = sigma * (1.0 + gate * (1.0 - sigma))
        ff = gate.shape[1]
        keep_ref[0, :, 0:ff] = (up * slope).astype(BF)
        keep_ref[0, :, ff : 2 * ff] = act.astype(BF)
        inner = (act * up).astype(BF)
        at = META - 32
        tails = [arrived[n][i, 32:48, 0:128].astype(F32) for n, i, _, _ in layout]
        pad = [jnp.zeros((8 - blocks, 128), F32)]
        wrow, srow = [
            jnp.concatenate(
                [jnp.where(h == 0, t[n : n + 1], t[n + 2 : n + 3]) for t in tails] + pad, axis=0
            ).astype(BF)
            for n in (at, at + 1)
        ]
        col8 = iota((owned, 8), 1)
        col = iota((owned, rows), 1)
        home8 = jnp.full((owned, 8), -1, I32)
        home = jnp.full((owned, rows), -1, I32)
        for r, (_, _, m, k) in enumerate(layout):
            first, second = (here_x - m) & 3, (here_y - k) & 3
            third_, fourth = (here_x - k) & 3, (here_y - m) & 3
            j = jnp.where(core == 0, first * LINE + second, third_ * LINE + fourth)
            home8 = jnp.where(col8 == r, j, home8)
            home = jnp.where(col >= r * WIN, j, home)
        owner = (third(iota((owned, 8), 0)) == home8).astype(BF)
        wrep = mm(owner, wrow)
        srep = mm(owner, srow)
        row = iota((owned, 128), 0)
        number = (row - SEQS * third(row) + 1).astype(F32)
        picked = jnp.where(srep == number, wrep, 0.0).astype(BF)
        place = iota((128, rows), 1)
        place = place - WIN * ((place * 683) >> 15)
        spread = (place == iota((128, rows), 0)).astype(BF)
        inside = third(iota((owned, rows), 0)) == home
        weights = jnp.where(inside, mm(picked, spread), 0.0).astype(BF)
        w_ref[0] = weights
        a = before_ref[...] + mm(weights, inner)
        if not last:
            a_ref[...] = a
            return
        high, low = split2(a)
        a_ref[...] = high
        both = mm(jnp.concatenate([high, low], axis=0), down_ref[0])
        total = both[:owned] + both[owned:]
        total = jnp.where(h == 0, total, total + acc_ref[...])
        acc_ref[...] = total

        @pl.when(h == 1)
        def _():
            for g in range(groups):
                for c in range(total.shape[1] // 128):
                    part_ref[g, c * SEQS : (c + 1) * SEQS, :] = total[
                        g * SEQS : (g + 1) * SEQS, c * 128 : (c + 1) * 128
                    ]

    run(e)


def pool_kernel(len_ref, pos_ref, recv_ref, sum_ref, out_ref, note_ref):
    groups, packed, _ = recv_ref.shape
    chunks = packed // SEQS
    total = recv_ref[0]
    for g in range(1, groups):
        total = total + recv_ref[g]
    note_ref[0:packed, :] = total
    total = jnp.concatenate([note_ref[c * SEQS : (c + 1) * SEQS, :] for c in range(chunks)], axis=1)
    row = iota((SEQS, 1), 0)
    inverse = jnp.zeros((SEQS, 1), F32)
    for s in range(SEQS):
        inverse = jnp.where(row == s, 1.0 / jnp.full((SEQS, 1), len_ref[s], I32).astype(F32), inverse)
    pooled = (total + sum_ref[0:SEQS, :]) * inverse
    scale = lax.rsqrt(jnp.sum(pooled * pooled, axis=1, keepdims=True) + norm_eps)
    positive = pos_ref[0]
    col = iota((1, 128), 1)
    note = jnp.where(col == 0, (positive >> 1) * SEQS + 1 + (positive & 1), 0)
    for s in range(SEQS):
        note = jnp.where(col == 1 + s, len_ref[s], note)
    note = note.astype(F32)
    for place, piece in enumerate(split3(scale)):
        piece = piece.astype(F32)
        for s in range(SEQS):
            note = jnp.where(col == 4 * (place + 1) + 1 + s, piece[s : s + 1], note)
    embed = pooled * scale
    for c in range(chunks):
        note_ref[c * SEQS : (c + 1) * SEQS, :] = embed[:, c * 128 : (c + 1) * 128]
    note_ref[packed:, :] = jnp.where(iota((NOTE, 128), 0) == 0, note, 0.0)
    value = note_ref[...].astype(BF)
    for g in range(groups):
        out_ref[g] = value


def contrast_kernel(at_ref, recv_ref, loss_ref, out_ref, all_ref, grad_ref, note_ref):
    groups = recv_ref.shape[0]
    packed = recv_ref.shape[1] - NOTE
    chunks = packed // SEQS
    owned = groups * SEQS
    me = at_ref[0]
    notes = []
    for g in range(groups):
        value = recv_ref[g].astype(F32)
        notes.append(value[packed : packed + 1])
        for c in range(chunks):
            all_ref[g * SEQS : (g + 1) * SEQS, c * 128 : (c + 1) * 128] = value[c * SEQS : (c + 1) * SEQS]
    notes = jnp.concatenate(notes, axis=0).astype(BF)

    def sort(shape, axis):
        place = iota(shape, axis)
        return place - SEQS * third(place)

    owner = (third(iota((owned, groups), 0)) == iota((owned, groups), 1)).astype(BF)
    notes = mm(owner, notes)
    lane = iota((owned, 128), 1)
    sub = sort((owned, 128), 0)
    target = jnp.sum(jnp.where(lane == 0, notes, 0.0), axis=1, keepdims=True)
    length = jnp.sum(jnp.where(lane == 1 + sub, notes, 0.0), axis=1, keepdims=True)
    pieces = jnp.logical_and(lane > 4, lane < 16)
    scale = jnp.sum(jnp.where(jnp.logical_and(pieces, (lane & 3) == 1 + sub), notes, 0.0), axis=1, keepdims=True)
    wide = all_ref[...]
    embed = wide.astype(BF)
    scores = mm(embed, embed, NT) * inv_temp
    passage = sort((owned, owned), 1) > 0
    total = jnp.log(jnp.sum(jnp.where(passage, jnp.exp(scores), 0.0), axis=1, keepdims=True))
    hit = (iota((owned, owned), 1).astype(F32) == target).astype(F32)
    losses = total - jnp.sum(hit * scores, axis=1, keepdims=True)
    wanted = iota((owned, 128), 0) == me * SEQS
    loss_ref[...] = jnp.sum(jnp.where(wanted, losses, 0.0), axis=0, keepdims=True)
    coeff = (jnp.where(passage, jnp.exp(scores - total), 0.0) - hit) * (loss_scale * inv_temp)
    coeff = jnp.where(sort((owned, owned), 0) == 0, coeff, 0.0)
    coeff = coeff + coeff.T
    three = mm(jnp.concatenate(split3(coeff), axis=0), embed)
    grad = three[:owned] + three[owned : 2 * owned] + three[2 * owned :]
    along = jnp.sum(wide * grad, axis=1, keepdims=True)
    grad = (grad - wide * along) * (scale / length)
    for g in range(groups):
        grad_ref[g] = grad[g * SEQS : (g + 1) * SEQS]
    own = grad_ref[me]
    for c in range(chunks):
        note_ref[c * SEQS : (c + 1) * SEQS, :] = own[:, c * 128 : (c + 1) * 128]
    for r in range(groups // 2):
        z = (((me >> 1) + (0, -2, 2, 4)[r // 2]) & (groups // 2 - 1)) ^ (r % 2)
        i = 2 * z + (me & 1)
        for h in range(2):
            here = pl.ds(pl.multiple_of((me ^ h) * 128, 128), 128)
            spot = packed + (2 * r + h) * SEQS
            note_ref[spot : spot + SEQS, :] = grad_ref[i, :, here]
    value = note_ref[...].astype(BF)
    for g in range(out_ref.shape[0]):
        out_ref[g] = value


def weight_parts(layout, core, arrived, e, pre, mine_ref, other_ref, spot):
    x = jnp.concatenate([window(arrived[n], i, e) for n, i in layout], axis=0)
    part = mm(x, pre, TN)
    half = part.shape[0] // 2
    first, second = part[:half], part[half:]
    mine_ref[0, spot] = jnp.where(core == 0, first, second).astype(BF)
    other_ref[0, spot] = jnp.where(core == 0, second, first).astype(BF)


def first_kernel(layout, arrays, parts, at_ref, recv_ref, down_ref, *refs):
    keeps, ws = refs[:parts], refs[parts : 2 * parts]
    arrived = refs[2 * parts : 2 * parts + arrays]
    pre_ref, mine_ref, other_ref, grad_ref = refs[2 * parts + arrays :]
    ff = down_ref.shape[1]

    def run(e):
        @pl.when(e == 0)
        def _():
            for g in range(recv_ref.shape[0]):
                value = recv_ref[g].astype(F32)
                for c in range(grad_ref.shape[1] // 128):
                    grad_ref[g * SEQS : (g + 1) * SEQS, c * 128 : (c + 1) * 128] = value[c * SEQS : (c + 1) * SEQS]
        back = mm(grad_ref[...].astype(BF), down_ref[0], NT)
        high, low = split2(back)
        two = jnp.concatenate([high, low], axis=0)
        start = 0
        for keep_ref, w_ref in zip(keeps, ws):
            weights = w_ref[0]
            end = start + weights.shape[1]
            inner = mm(jnp.concatenate([weights, weights], axis=0), two, TN)
            pre_ref[0, start:end, 0:ff] = (inner * keep_ref[0, :, 0:ff].astype(F32)).astype(BF)
            pre_ref[0, start:end, ff : 2 * ff] = (inner * keep_ref[0, :, ff : 2 * ff].astype(F32)).astype(BF)
            start = end
        weight_parts(layout, at_ref[2], arrived, e, pre_ref[0], mine_ref, other_ref, 0)

    run(pl.program_id(0))


def more_kernel(layout, arrays, at_ref, pre_ref, *refs):
    for e in range(pre_ref.shape[0]):
        weight_parts(layout, at_ref[2], refs[:arrays], e, pre_ref[e], *refs[arrays:], e)


def down_kernel(recv_ref, *refs):
    pairs, (mine_ref, other_ref, grad_ref) = refs[:4], refs[4:]
    groups = recv_ref.shape[0]
    owned = pairs[0].shape[1]
    both = 2 * owned
    packed = recv_ref.shape[1] - 16 * SEQS
    for g in range(groups):
        value = recv_ref[g].astype(F32)
        for r in range(8):
            for h in range(2):
                spot = packed + (2 * r + h) * SEQS
                row = r * owned + g * SEQS
                grad_ref[row : row + SEQS, h * 128 : (h + 1) * 128] = value[spot : spot + SEQS]
    grad = grad_ref[...].astype(BF)
    total = sum(
        mm(ref[...].reshape(both, -1), grad[n * both : (n + 1) * both], TN) for n, ref in enumerate(pairs)
    )
    mine_ref[...] = total[:, :128]
    other_ref[...] = total[:, 128:]


def body(hidden, w_gate, w_up, w_down, expert_ids, route_weight, seq_len, positive):
    dp, ep = ("z", "core"), ("x", "y")
    tok, width = hidden.shape
    local, _, ff = w_gate.shape
    groups = lax.axis_size(ep)
    members = lax.axis_size(dp)
    top = expert_ids.shape[1]
    length = tok // SEQS
    owned = groups * SEQS
    packed = SEQS * width // 128
    rows = groups * WIN
    me = lax.axis_index(dp).astype(I32).reshape(1)
    smem = pl.BlockSpec(memory_space=pltpu.SMEM)

    def limit(mib):
        return pltpu.CompilerParams(vmem_limit_bytes=mib * 1024 * 1024)

    big = pltpu.CompilerParams(vmem_limit_bytes=50 * 1024 * 1024)

    at = jnp.stack([lax.axis_index(a) for a in ("x", "y", "core", "z")]).astype(I32)
    vmem = pl.BlockSpec(memory_space=pltpu.VMEM)
    message, hidden_sum = pl.pallas_call(
        functools.partial(prepare_kernel, length),
        out_shape=(
            jax.ShapeDtypeStruct((tok + NOTE, width), BF),
            jax.ShapeDtypeStruct((8, width), F32),
        ),
        in_specs=[smem, vmem, vmem, vmem],
        out_specs=(vmem, vmem),
        name="prepare",
    )(seq_len, expert_ids.T, route_weight.T, hidden)

    def ahead(value, k, turned):
        pairs = []
        for core in range(2):
            for x in range(LINE):
                for y in range(LINE):
                    to = ((x + k) % LINE, y) if core == turned else (x, (y + k) % LINE)
                    pairs.append(((core * LINE + x) * LINE + y, (core * LINE + to[0]) * LINE + to[1]))
        return lax.ppermute(value, ("core", "x", "y"), pairs)

    def select(name, halves, *messages):
        count = 1 if halves else 3
        sizes = (1, 1, 1, 1) if halves else (3, 3, 2, 3, 1)
        return pl.pallas_call(
            functools.partial(select_kernel, halves),
            grid=(count,),
            out_shape=[jax.ShapeDtypeStruct((n, PART, width), BF) for n in sizes],
            in_specs=[smem] + [pl.BlockSpec(v.shape, lambda m: (0, 0)) for v in messages],
            out_specs=[
                pl.BlockSpec((1, PART, width), lambda m, n=n: (jnp.minimum(m, n - 1), 0, 0)) for n in sizes
            ],
            cost_estimate=pl.CostEstimate(
                flops=count * LINE * PART * 2 * tok * width,
                bytes_accessed=count * 2 * width * (tok + LINE * PART),
                transcendentals=0,
            ),
            compiler_params=limit(28),
            name=name,
        )(at, *messages)

    cut = (tok + NOTE) // 2
    one, three = ahead(message, 1, 0), ahead(message, 3, 0)
    two = ahead(one[:cut], 1, 0), ahead(three[cut:], 3, 0)
    here, plus, relay, minus, back = select("select_near", False, message, one, three)
    plus, minus = ahead(plus, 1, 1), ahead(minus, 3, 1)
    relay, back = ahead(relay, 1, 1), ahead(back, 3, 1)

    def near_blocks(array, k):
        return [(array, i, m, k) for i, m in enumerate((0, 1, 3))]

    keeps, weights = [], []

    def forward(part, last, arrays, layout, summed):
        rows = len(layout) * WIN
        matrix = pl.BlockSpec((1, width, ff), lambda e: (e, 0, 0))
        sums = pl.BlockSpec((owned, ff), lambda e: (0, e))
        out_shape = [
            jax.ShapeDtypeStruct((owned, local * ff), BF if last else F32),
            pltpu.HBM((local, rows, 2 * ff), BF),
            pltpu.HBM((local, owned, rows), BF),
        ]
        out_specs = [
            sums,
            pl.BlockSpec((1, rows, 2 * ff), lambda e: (e, 0, 0)),
            pl.BlockSpec((1, owned, rows), lambda e: (e, 0, 0)),
        ]
        in_specs = [smem] + [pl.BlockSpec(v.shape, lambda e: (0, 0, 0)) for v in arrays] + [matrix, matrix]
        operands = [at, *arrays, w_gate, w_up]
        if last:
            in_specs.append(pl.BlockSpec((1, ff, width), lambda e: (e, 0, 0)))
            operands.append(w_down)
            out_shape.append(jax.ShapeDtypeStruct((groups, packed, 128), F32))
            out_specs.append(pl.BlockSpec((groups, packed, 128), lambda e: (0, 0, 0)))
        results = pl.pallas_call(
            functools.partial(forward_kernel, layout, last),
            grid=(local,),
            out_shape=out_shape,
            in_specs=in_specs + [sums],
            out_specs=out_specs,
            scratch_shapes=[pltpu.VMEM((owned, width), F32)] if last else [],
            cost_estimate=pl.CostEstimate(
                flops=local * rows * 4 * width * ff,
                bytes_accessed=local * 4 * width * ff + 4 * rows * width,
                transcendentals=local * rows * ff,
            ),
            compiler_params=limit(32),
            name="forward_%d" % part,
        )(*operands, summed)
        keeps.append(results[1])
        weights.append(results[2])
        return results

    layouts = [near_blocks(0, 0), near_blocks(0, 1) + near_blocks(1, 3)]
    groups_of = [(here,), (plus, minus)]
    summed = forward(0, False, groups_of[0], layouts[0], jnp.zeros((owned, local * ff), F32))[0]
    two, summed = lax.optimization_barrier((two, summed))
    far_here, far_plus, far_back, far_minus = select("select_far", True, *two)
    far_plus, far_minus, far_back = ahead(far_plus, 1, 1), ahead(far_minus, 3, 1), ahead(far_back, 3, 1)
    summed = forward(1, False, groups_of[1], layouts[1], summed)[0]
    relay, back, far_back, summed = lax.optimization_barrier((relay, back, far_back, summed))
    relay, back, far_back = ahead(relay, 1, 1), ahead(back, 3, 1), ahead(far_back, 3, 1)
    groups_of.append((relay, back, far_plus, far_back, far_minus, far_here))
    layouts.append(
        [(0, 0, 0, 2), (0, 1, 1, 2), (1, 0, 3, 2), (2, 0, 2, 1), (3, 0, 2, 2), (4, 0, 2, 3), (5, 0, 2, 0)]
    )
    results = forward(2, True, groups_of[2], layouts[2], summed)
    summed = results[0]
    partial = results[3]
    rows = groups * WIN
    arrived, layout = [], []
    for arrays, blocks in zip(groups_of, layouts):
        layout += [(len(arrived) + n, i) for n, i, _, _ in blocks]
        arrived += arrays

    returned = lax.all_to_all(partial, ep, split_axis=0, concat_axis=0, tiled=True)

    ring = lax.axis_size("z")

    def across(value, k):
        return lax.ppermute(value, "z", [(i, i ^ k) for i in range(ring)])

    def along(value, k):
        return lax.ppermute(value, "z", [(i, (i + k) % ring) for i in range(ring)])

    one_sum = across(summed, 1)
    returned, one_sum = lax.optimization_barrier((returned, one_sum))
    pair = jnp.stack([summed, one_sum])

    pooled = pl.pallas_call(
        pool_kernel,
        out_shape=jax.ShapeDtypeStruct((members, packed + NOTE, 128), BF),
        in_specs=[smem, smem, vmem, vmem],
        out_specs=vmem,
        scratch_shapes=[pltpu.VMEM((packed + NOTE, 128), F32)],
        compiler_params=limit(8),
        name="pool",
    )(seq_len, positive, returned, hidden_sum)
    column = lax.all_to_all(pooled, dp, split_axis=0, concat_axis=0, tiled=True)
    below, above = along(pair, 2), along(pair, -2)
    column, below, above = lax.optimization_barrier((column, below, above))
    far_sums = along(below, 2)

    noted = packed + members * SEQS
    loss, note = pl.pallas_call(
        contrast_kernel,
        out_shape=(
            jax.ShapeDtypeStruct((1, 128), F32),
            jax.ShapeDtypeStruct((groups, noted, 128), BF),
        ),
        in_specs=[smem, vmem],
        out_specs=(vmem, vmem),
        scratch_shapes=[
            pltpu.VMEM((members * SEQS, width), F32),
            pltpu.VMEM((members, SEQS, width), F32),
            pltpu.VMEM((noted, 128), F32),
        ],
        compiler_params=limit(12),
        name="contrast",
    )(me, column)
    spread = lax.all_to_all(note, ep, split_axis=0, concat_axis=0, tiled=True)
    spread, far_sums = lax.optimization_barrier((spread, far_sums))
    cols = width // ring
    piece = (local, cols // 2, 2 * ff)

    def shard_spec(order):
        return [
            pl.BlockSpec((v.shape[0], PART, cols), lambda i, at: (0, 0, (at[3] + order(i)) & (ring - 1)))
            for v in arrived
        ]

    def parts_spec():
        return pl.BlockSpec((1,) + piece, lambda i, at: (i, 0, 0, 0))

    def cost(shards, extra=0):
        flops = shards * local * 2 * rows * cols * 2 * ff
        return pl.CostEstimate(flops=flops, bytes_accessed=shards * 4 * local * rows * cols + extra, transcendentals=0)

    pre, mine, other = pl.pallas_call(
        functools.partial(first_kernel, layout, len(arrived), len(keeps)),
        grid_spec=pltpu.PrefetchScalarGridSpec(
            num_scalar_prefetch=1,
            grid=(local,),
            in_specs=[
                pl.BlockSpec((groups, noted, 128), lambda i, at: (0, 0, 0)),
                pl.BlockSpec((1, ff, width), lambda i, at: (i, 0, 0)),
            ]
            + [pl.BlockSpec((1,) + v.shape[1:], lambda i, at: (i, 0, 0)) for v in keeps + weights]
            + shard_spec(lambda i: 4),
            out_specs=[
                pl.BlockSpec((1, rows, 2 * ff), lambda i, at: (i, 0, 0)),
                pl.BlockSpec((1, 1) + piece[1:], lambda i, at: (0, i, 0, 0)),
                pl.BlockSpec((1, 1) + piece[1:], lambda i, at: (0, i, 0, 0)),
            ],
            scratch_shapes=[pltpu.VMEM((owned, width), F32)],
        ),
        out_shape=(
            jax.ShapeDtypeStruct((local, rows, 2 * ff), BF),
            jax.ShapeDtypeStruct((1,) + piece, BF),
            jax.ShapeDtypeStruct((1,) + piece, BF),
        ),
        cost_estimate=cost(1, 16 * 1024 * 1024),
        compiler_params=big,
        name="first_parts",
    )(at, spread, w_down, *keeps, *weights, *arrived)

    def more(shards, order, name):
        return pl.pallas_call(
            functools.partial(more_kernel, layout, len(arrived)),
            grid_spec=pltpu.PrefetchScalarGridSpec(
                num_scalar_prefetch=1,
                grid=(shards,),
                in_specs=[pl.BlockSpec((local, rows, 2 * ff), lambda i, at: (0, 0, 0))] + shard_spec(order),
                out_specs=[parts_spec(), parts_spec()],
            ),
            out_shape=[jax.ShapeDtypeStruct((shards,) + piece, BF)] * 2,
            cost_estimate=cost(shards),
            compiler_params=big,
            name=name,
        )(at, pre, *arrived)

    def swap(value):
        return lax.ppermute(value, "core", [(0, 1), (1, 0)])

    def total(*values):
        return sum(v.astype(F32) for v in values)

    theirs = swap(other)
    held, sent = more(2, lambda i: 3 + 2 * i, "parts_three")
    up, down = total(mine[0, 0], theirs[0, 0]).astype(BF), total(mine[0, 1], theirs[0, 1]).astype(BF)
    up, down, pre, sent = lax.optimization_barrier((up, down, pre, sent))
    up, down, got = along(up, 1), along(down, -1), swap(sent)
    later = more(2, lambda i: 2 + 4 * i, "parts_two")
    up = jnp.stack([total(held[0, 0], got[0, 0], up), total(held[0, 1], got[0, 1])]).astype(BF)
    down = jnp.stack([total(held[1, 0], got[1, 0]), total(held[1, 1], got[1, 1], down)]).astype(BF)
    up, down, pre, later = lax.optimization_barrier((up, down, pre, later))
    held, sent = later
    up, down, got = along(up, 1), along(down, -1), swap(sent)
    later = more(3, lambda i: jnp.where(i == 0, 1, 7 * (2 - i)), "parts_one")
    up = total(held[0], got[0], up).astype(BF)
    down = total(held[1], got[1], down).astype(BF)
    up, down, later, far_sums = lax.optimization_barrier((up, down, later, far_sums))
    held, sent = later
    up, down, got = along(up, 1), along(down, -1), swap(sent)
    up = total(held[0], got[0], up).astype(BF)
    down = total(held[1], got[1], down).astype(BF)
    up, down = lax.optimization_barrier((up, down))
    up, down = along(up, 1), along(down, -1)
    grad_gate, grad_up = [
        total(held[2, :, :, s], got[2, :, :, s], up[:, :, s], down[:, :, s])
        for s in (slice(0, ff), slice(ff, 2 * ff))
    ]
    down_mine, down_other = pl.pallas_call(
        down_kernel,
        out_shape=[jax.ShapeDtypeStruct((local * ff, 128), F32)] * 2,
        in_specs=[vmem] * 5,
        out_specs=[vmem, vmem],
        scratch_shapes=[pltpu.VMEM((ring * owned, 256), F32)],
        cost_estimate=pl.CostEstimate(
            flops=2 * ring * owned * local * ff * 256, bytes_accessed=4 * 1024 * 1024, transcendentals=0
        ),
        compiler_params=limit(12),
        name="down",
    )(spread, pair, below, above, far_sums)
    grad_down = (down_mine + swap(down_other)).reshape(local, ff, 128)
    return (
        loss[0, :1],
        grad_gate,
        grad_up,
        grad_down,
    )


def solution(mesh):
    mesh = Mesh(mesh.devices.reshape(8, 2, 4, 4), ("z", "core", "x", "y"))
    dp, ep = ("z", "core"), ("x", "y")
    tokens = P(dp + ep)
    placed = (
        P(dp + ep, None),
        P(ep, None, None),
        P(ep, None, None),
        P(ep, None, None),
        P(dp + ep, None),
        P(dp + ep, None),
        tokens,
        tokens,
    )
    return jax.shard_map(
        body,
        mesh=mesh,
        in_specs=placed,
        out_specs=(tokens, P(ep, dp, None), P(ep, dp, None), P(ep, None, dp)),
        check_vma=False,
    )
```
